32 devices in a mesh: group: 2 (over x), out: 8 (over z, y), inp: 2 (over core).
Axes of the slice: x: 2, y: 2, z: 4, core: 2. Of those that a mesh axis runs over, the one named last changes fastest.
Arguments:
- tokens: bfloat16 [2, 128, 8192], P(None, ('group', 'out')), parts along dimension 1, may hold values from -6 to 6
- norm_gain: float32 [8192], replicated, may hold values from 0.1 to 1.9
- query_weight: bfloat16 [8192, 8192], P('inp', 'out'), may hold values from -0.0625 to 0.0625
- key_matrix: bfloat16 [8192, 1024], P('inp', 'out'), may hold values from -0.0625 to 0.0625
- value_matrix: bfloat16 [8192, 1024], P('inp', 'out'), may hold values from -0.0625 to 0.0625
- output_weight: bfloat16 [8192, 8192], P('inp', 'out'), may hold values from -0.0625 to 0.0625
- cache_keys: bfloat16 [128, 512, 8, 128], P(('group', 'out'), None, 'inp'), parts along dimension 0, may hold values from -400 to 400
- stored_cache_values: bfloat16 [128, 512, 8, 128], P(('group', 'out'), None, 'inp'), parts along dimension 0, may hold values from -16 to 16
- lengths: int32 [128], P(('group', 'out')), parts along dimension 0, may hold values from 1 to 512, as said below
- positions: int32 [128], P(('group', 'out')), parts along dimension 0, may hold values from 512 to 8191
Outputs:
- mixed: bfloat16 [2, 128, 8192], P(None, ('group', 'out')), parts along dimension 1
The draws below stay inside these ranges and needn't reach their ends.
There are 2 independent parts, one for each index of `group`. The reference program is written for one: setup_inputs(seed, part) draws one part's arguments, and reference() takes and returns one part's arrays. A program takes and returns all parts, laid end to end along the dimension named above; an argument that names none is the same for every part. Nothing has to cross between parts.
Inputs may be any that keep to these rules, and one draw needn't show every extreme that they name: `lengths`: each row's valid cache entries start at slot 0; in every draw some row holds all 512 and some row holds 1.
All inputs are finite; a program needn't handle non-finite values.
Results may differ from the reference program's by a relative error of at most 0.0065.
The reference program's roundings to bfloat16 on the way count: a program that leaves them out, or rounds other values in their place, can miss the bound.
Values may be sent and summed in bfloat16 or wider, within the bound.
No kernel may reach another device: no remote copies, remote signals or barrier semaphores. Data moves between devices by JAX's collectives and lax.ppermute only.
A program may use at most 128 MiB of HBM per device.

```python
import math
import jax
import jax.numpy as jnp
from jax import lax

MODEL_WIDTH = 8192
HQ = 64
KEY_VALUE_HEADS = 8
HEAD_SIZE = 128
CACHE_SLOTS = 512
DECODED_ROWS = 64


def draw_lengths(key, part):
    key = jax.random.fold_in(key, 11)
    leading_key_row, trailing_key_row, third_key, fourth_key = jax.random.split(key, 4)
    exponent = jax.random.randint(leading_key_row, (DECODED_ROWS,), 0, 3)
    spans = jnp.right_shift(jnp.full((DECODED_ROWS,), CACHE_SLOTS, jnp.int32), exponent)
    counts = 1 + jax.random.randint(trailing_key_row, (DECODED_ROWS,), 0, spans)
    counts = jnp.minimum(counts, CACHE_SLOTS)
    full_row = jax.random.randint(third_key, (), 0, DECODED_ROWS)
    single_row = (full_row + 1 + jax.random.randint(fourth_key, (), 0, DECODED_ROWS - 1)) % DECODED_ROWS
    row_ids = jnp.arange(DECODED_ROWS)
    counts = jnp.where(row_ids == full_row, CACHE_SLOTS, jnp.where(row_ids == single_row, 1, counts))
    return counts.astype(jnp.int32)


def draw_cache_keys(key, part):
    key = jax.random.fold_in(key, 5)
    leading_key_row = jax.random.fold_in(key, 0)
    sampled_example = jax.random.truncated_normal(leading_key_row, -4.0, 4.0, (DECODED_ROWS, CACHE_SLOTS, KEY_VALUE_HEADS, HEAD_SIZE), jnp.float32)
    return sampled_example.astype(jnp.bfloat16)


def touch_ends(result, rng, low, largest):
    place = [jax.random.randint(jax.random.fold_in(rng, axis), (), 0, length) for axis, length in enumerate(result.shape)]
    main_axis = result.shape.index(max(result.shape))
    next_to = place[:main_axis] + [(place[main_axis] + 1) % result.shape[main_axis]] + place[main_axis + 1:]
    return result.at[tuple(place)].set(low).at[tuple(next_to)].set(largest)


def shard_levels(stream_key, dims, cuts, least, high):
    level = 1.0
    for axis_at, blocks in cuts:
        steps = jax.random.uniform(jax.random.fold_in(jax.random.fold_in(stream_key, 6), axis_at), (blocks,), jnp.float32, least / len(cuts), high / len(cuts))
        level = level * jnp.repeat(jnp.exp(steps), dims[axis_at] // blocks).reshape((-1,) + (1,) * (len(dims) - 1 - axis_at))
    return level


def bell_draw(own_key, shape, scale, bound, cuts=(), held_as=jnp.bfloat16):
    level = shard_levels(own_key, shape, cuts, -0.22, 0.18) if cuts else 1.0
    entries = jax.random.normal(own_key, shape, jnp.float32) * scale * level
    return jnp.minimum(jnp.maximum(entries, -bound), bound).astype(held_as)


def setup_inputs(seed: int = 0, part: int = 0) -> dict:
    arg_keys = jax.random.split(jax.random.key(seed), 11)
    part_keys = jax.random.split(jax.random.fold_in(arg_keys[10], part), 11)
    tokens = bell_draw(part_keys[0], (2, DECODED_ROWS, MODEL_WIDTH), 1.0, 6.0, ((1, 8),))
    norm_gain = jnp.clip(1.0 + 0.18 * jax.random.normal(arg_keys[1], (MODEL_WIDTH,), jnp.float32), 0.1, 1.9)
    query_weight = bell_draw(arg_keys[2], (MODEL_WIDTH, HQ * HEAD_SIZE), MODEL_WIDTH ** -0.5, 0.0625, ((0, 2), (1, 8)))
    key_matrix = bell_draw(arg_keys[3], (MODEL_WIDTH, KEY_VALUE_HEADS * HEAD_SIZE), MODEL_WIDTH ** -0.5, 0.0625, ((0, 2), (1, 8)))
    value_matrix = bell_draw(arg_keys[4], (MODEL_WIDTH, KEY_VALUE_HEADS * HEAD_SIZE), MODEL_WIDTH ** -0.5, 0.0625, ((0, 2), (1, 8)))
    output_weight = bell_draw(arg_keys[5], (HQ * HEAD_SIZE, MODEL_WIDTH), (HQ * HEAD_SIZE) ** -0.5, 0.0625, ((0, 2), (1, 8)))
    cache_keys = draw_cache_keys(jax.random.fold_in(jax.random.fold_in(arg_keys[10], part), 71), part)
    stored_cache_values = bell_draw(part_keys[7], (DECODED_ROWS, CACHE_SLOTS, KEY_VALUE_HEADS, HEAD_SIZE), 4.0, 16.0, ((0, 8), (2, 2)))
    lengths = draw_lengths(jax.random.fold_in(jax.random.fold_in(arg_keys[10], part), 71), part)
    positions = touch_ends(jax.random.randint(part_keys[9], (DECODED_ROWS,), CACHE_SLOTS, 8192), jax.random.fold_in(part_keys[9], 1), CACHE_SLOTS, 8191).astype(jnp.int32)
    return {"tokens": tokens, "norm_gain": norm_gain, "query_weight": query_weight, "key_matrix": key_matrix, "value_matrix": value_matrix, "output_weight": output_weight, "cache_keys": cache_keys, "stored_cache_values": stored_cache_values, "lengths": lengths, "positions": positions}


def rms_normed(tokens, gain):
    values = tokens.astype(jnp.float32)
    factor = lax.rsqrt(lax.optimization_barrier(jnp.mean(values * values, axis=-1, keepdims=True)) + 1e-05)
    return (values * factor * gain).astype(jnp.bfloat16)

def rotate(heads, position):
    head_size = heads.shape[-1]
    half_size = head_size // 2
    frequency = jnp.exp(-math.log(500000.0) * 2.0 * jnp.arange(half_size, dtype=jnp.float32) / head_size)
    angles = position.astype(jnp.float32)[..., None, None] * frequency
    cosine = jnp.cos(angles)
    sine_part = jnp.sin(angles)
    leading = heads[..., :half_size]
    trailing = heads[..., half_size:]
    return jnp.concatenate([leading * cosine - trailing * sine_part, trailing * cosine + leading * sine_part], axis=-1)

def attend_one(queries, new_keys, new_values, cache_keys, stored_cache_values, lengths):
    count_of_rows, head_count, head_size = queries.shape
    key_heads = cache_keys.shape[2]
    grouped = queries.astype(jnp.float32).reshape(count_of_rows, key_heads, head_count // key_heads, head_size)
    factor = head_size ** (-0.5)
    cached = jnp.einsum('rkgd,rckd->rkgc', grouped, cache_keys.astype(jnp.float32)) * factor
    visible = jnp.arange(cache_keys.shape[1])[None, :] < lengths[:, None]
    cached = jnp.where(visible[:, None, None, :], cached, -jnp.inf)
    fresh_scores = jnp.einsum('rkgd,nrkd->rkgn', grouped, new_keys.astype(jnp.float32)) * factor
    highest = jnp.maximum(lax.optimization_barrier(jnp.max(cached, axis=-1)), lax.optimization_barrier(jnp.max(fresh_scores, axis=-1)))
    cached_exp = jnp.exp(cached - highest[..., None])
    fresh_exp = jnp.exp(fresh_scores - highest[..., None])
    totals = lax.optimization_barrier(jnp.sum(cached_exp, axis=-1)) + lax.optimization_barrier(jnp.sum(fresh_exp, axis=-1))
    cached_prob = (cached_exp / totals[..., None]).astype(jnp.bfloat16)
    fresh_prob = (fresh_exp / totals[..., None]).astype(jnp.bfloat16)
    attended = jnp.einsum('rkgc,rckd->rkgd', cached_prob.astype(jnp.float32), stored_cache_values.astype(jnp.float32))
    attended = attended + jnp.einsum('rkgn,nrkd->rkgd', fresh_prob.astype(jnp.float32), new_values.astype(jnp.float32))
    return attended.reshape(count_of_rows, head_count * head_size).astype(jnp.bfloat16)

def reference(tokens, norm_gain, query_weight, key_matrix, value_matrix, output_weight, cache_keys, stored_cache_values, lengths, positions):
    count_of_rows = tokens.shape[1]
    key_list = []
    value_list = []
    results = []
    for token_step in range(2):
        normalized_input = rms_normed(tokens[token_step], norm_gain)
        queries = jnp.dot(normalized_input, query_weight, preferred_element_type=jnp.float32).reshape(count_of_rows, HQ, HEAD_SIZE)
        incoming_keys = jnp.dot(normalized_input, key_matrix, preferred_element_type=jnp.float32).reshape(count_of_rows, KEY_VALUE_HEADS, HEAD_SIZE)
        incoming_values = jnp.dot(normalized_input, value_matrix, preferred_element_type=jnp.float32).reshape(count_of_rows, KEY_VALUE_HEADS, HEAD_SIZE)
        placed = positions + token_step
        queries = rotate(queries, placed).astype(jnp.bfloat16)
        key_list.append(rotate(incoming_keys, placed).astype(jnp.bfloat16))
        value_list.append(incoming_values.astype(jnp.bfloat16))
        attended = attend_one(queries, jnp.stack(key_list), jnp.stack(value_list), cache_keys, stored_cache_values, lengths)
        results.append(jnp.dot(attended, output_weight, preferred_element_type=jnp.float32).astype(jnp.bfloat16))
    return jnp.stack(results)
```

```python
import math

import jax
import jax.numpy as jnp
from jax import lax
from jax.sharding import PartitionSpec as P

HEAD_SIZE = 128


def rms_normed(tokens, gain):
    values = tokens.astype(jnp.float32)
    factor = lax.rsqrt(jnp.mean(values * values, axis=-1, keepdims=True) + 1e-05)
    return (values * factor * gain).astype(jnp.bfloat16)


def rotate(heads, position):
    head_size = heads.shape[-1]
    half_size = head_size // 2
    frequency = jnp.exp(
        -math.log(500000.0) * 2.0 * jnp.arange(half_size, dtype=jnp.float32) / head_size
    )
    angles = position.astype(jnp.float32)[..., None, None] * frequency
    cosine = jnp.cos(angles)
    sine_part = jnp.sin(angles)
    leading = heads[..., :half_size]
    trailing = heads[..., half_size:]
    return jnp.concatenate(
        [leading * cosine - trailing * sine_part, trailing * cosine + leading * sine_part], axis=-1
    )


def attend_one(queries, new_keys, new_values, cache_keys, stored_cache_values, lengths):
    count_of_rows, head_count, head_size = queries.shape
    key_heads = cache_keys.shape[2]
    grouped = queries.reshape(count_of_rows, key_heads, head_count // key_heads, head_size)
    factor = head_size ** (-0.5)
    cached = (
        jnp.einsum("rkgd,rckd->rkgc", grouped, cache_keys, preferred_element_type=jnp.float32)
        * factor
    )
    visible = jnp.arange(cache_keys.shape[1])[None, :] < lengths[:, None]
    cached = jnp.where(visible[:, None, None, :], cached, -jnp.inf)
    fresh_scores = (
        jnp.einsum("rkgd,nrkd->rkgn", grouped, new_keys, preferred_element_type=jnp.float32)
        * factor
    )
    highest = jnp.maximum(jnp.max(cached, axis=-1), jnp.max(fresh_scores, axis=-1))
    cached_exp = jnp.exp(cached - highest[..., None])
    fresh_exp = jnp.exp(fresh_scores - highest[..., None])
    totals = jnp.sum(cached_exp, axis=-1) + jnp.sum(fresh_exp, axis=-1)
    cached_prob = (cached_exp / totals[..., None]).astype(jnp.bfloat16)
    fresh_prob = (fresh_exp / totals[..., None]).astype(jnp.bfloat16)
    attended = jnp.einsum(
        "rkgc,rckd->rkgd", cached_prob, stored_cache_values, preferred_element_type=jnp.float32
    )
    attended = attended + jnp.einsum(
        "rkgn,nrkd->rkgd", fresh_prob, new_values, preferred_element_type=jnp.float32
    )
    return attended.reshape(count_of_rows, head_count * head_size).astype(jnp.bfloat16)


def project(normalized_input, query_weight, key_matrix, value_matrix, positions, first_step):
    out_count = lax.axis_size("out")
    inp_count = lax.axis_size("inp")
    inp_index = lax.axis_index("inp")
    step_count = normalized_input.shape[0]
    row_local = normalized_input.shape[1]
    feature_width = normalized_input.shape[2] // inp_count
    own_slice = lax.dynamic_slice_in_dim(
        normalized_input, inp_index * feature_width, feature_width, 2
    )
    query_cols = query_weight.shape[1]
    key_cols = key_matrix.shape[1]
    block_width = query_cols + 2 * key_cols
    shard_rows = lax.all_gather(own_slice, "out", axis=1, tiled=True)
    partials = jnp.concatenate(
        [
            jnp.dot(shard_rows, weight, preferred_element_type=jnp.float32)
            for weight in (query_weight, key_matrix, value_matrix)
        ],
        axis=-1,
    )
    totals = lax.psum(partials, "inp")
    regrouped = lax.all_to_all(totals, "out", split_axis=1, concat_axis=2, tiled=True)
    regrouped = regrouped.reshape(step_count, row_local, out_count, block_width)
    block_count = out_count // inp_count
    summed = lax.dynamic_slice_in_dim(regrouped, inp_index * block_count, block_count, 2)
    query_part = summed[..., :query_cols].reshape(step_count, row_local, -1, HEAD_SIZE)
    key_part = summed[..., query_cols : query_cols + key_cols].reshape(
        step_count, row_local, -1, HEAD_SIZE
    )
    value_part = summed[..., query_cols + key_cols :].reshape(step_count, row_local, -1, HEAD_SIZE)
    placed = positions[None, :] + (first_step + jnp.arange(step_count, dtype=jnp.int32))[:, None]
    queries = rotate(query_part, placed).astype(jnp.bfloat16)
    incoming_keys = rotate(key_part, placed).astype(jnp.bfloat16)
    incoming_values = value_part.astype(jnp.bfloat16)
    return (queries, incoming_keys, incoming_values)


def mix_out(attended, output_weight):
    partials = jnp.dot(
        lax.all_gather(attended, "out", axis=1, tiled=True),
        output_weight,
        preferred_element_type=jnp.float32,
    )
    totals = lax.psum(partials, "inp")
    return lax.all_to_all(
        totals.astype(jnp.bfloat16), "out", split_axis=1, concat_axis=2, tiled=True
    )


def exchange_orders(step):
    return {"far": (4, 4), "near": (2, 1), "last": (1, 2)}[step]


def swap_blocks(block, step):
    flips = exchange_orders(step)
    pairs = [(2 * o + i, 2 * (o ^ flips[i]) + i) for o in range(8) for i in range(2)]
    return lax.ppermute(block, ("out", "inp"), pairs)


def gather_blocks(block):
    far = swap_blocks(block, "far")
    near = swap_blocks(block, "near")
    last = swap_blocks(block, "last")
    near_last = swap_blocks(near, "last")
    far_near = swap_blocks(far, "near")
    far_last = swap_blocks(far, "last")
    far_near_last = swap_blocks(far_near, "last")
    return (block, near, last, near_last), (far, far_near, far_last, far_near_last)


def swap_cores(block):
    return lax.ppermute(block, "inp", [(0, 1), (1, 0)])


def offset_of(core, place):
    return (0, 2, 1, 3)[place] if core == 0 else place


def hand_out(blocks):
    received = []
    for place, block in enumerate(blocks):
        pairs = []
        for o in range(8):
            for i in range(2):
                target = o ^ (4 * i) ^ offset_of(i, place)
                pairs.append((2 * o + i, 2 * target + o // 4))
        received.append(lax.ppermute(block, ("out", "inp"), pairs))
    return received


def in_order(received):
    own_out = lax.axis_index("out")
    own_core = lax.axis_index("inp")
    crossed = (own_out // 4) ^ own_core
    stacked = jnp.stack(received)
    ordered = []
    for column in range(4):
        offset = column ^ (own_out % 4)
        swapped = jnp.where((offset == 1) | (offset == 2), 3 - offset, offset)
        place = jnp.where(crossed == 0, swapped, offset)
        ordered.append(lax.dynamic_index_in_dim(stacked, place, 0, keepdims=False))
    return ordered


def pair_summed(lower, upper, multiply):
    core = lax.axis_index("inp")
    lower = jnp.concatenate(lower)
    upper = jnp.concatenate(upper)
    given = multiply(jnp.where(core == 0, upper, lower))
    kept = multiply(jnp.where(core == 0, lower, upper))
    count = kept.shape[0] // 4
    arrived = swap_cores(given)
    arrived = arrived.reshape(4, count, -1)
    arrived = jnp.stack([arrived[0], arrived[2], arrived[1], arrived[3]])
    return kept.reshape(arrived.shape) + arrived


def attend_both(queries, new_keys, new_values, cache_keys, cache_values, lengths):
    factor = HEAD_SIZE ** (-0.5)
    steps = queries.shape[1]
    cached = jnp.einsum("ktrgd,rckd->rktgc", queries, cache_keys, preferred_element_type=jnp.float32) * factor
    visible = jnp.arange(cache_keys.shape[1])[None, :] < lengths[:, None]
    cached = jnp.where(visible[:, None, None, None, :], cached, -jnp.inf)
    fresh = jnp.einsum("ktrgd,knrd->rktgn", queries, new_keys, preferred_element_type=jnp.float32) * factor
    causal = jnp.arange(steps)[:, None] >= jnp.arange(steps)[None, :]
    fresh = jnp.where(causal[None, None, :, None, :], fresh, -jnp.inf)
    highest = jnp.maximum(jnp.max(cached, axis=-1), jnp.max(fresh, axis=-1))
    cached_exp = jnp.exp(cached - highest[..., None])
    fresh_exp = jnp.exp(fresh - highest[..., None])
    totals = jnp.sum(cached_exp, axis=-1) + jnp.sum(fresh_exp, axis=-1)
    cached_prob = (cached_exp / totals[..., None]).astype(jnp.bfloat16)
    fresh_prob = (fresh_exp / totals[..., None]).astype(jnp.bfloat16)
    attended = jnp.einsum("rktgc,rckd->trkgd", cached_prob, cache_values, preferred_element_type=jnp.float32)
    attended = attended + jnp.einsum("rktgn,knrd->trkgd", fresh_prob, new_values, preferred_element_type=jnp.float32)
    return attended.astype(jnp.bfloat16)


def eight_chip_body(
    tokens, norm_gain, query_weight, key_matrix, value_matrix, output_weight, cache_keys, cache_values, lengths, positions
):
    steps, rows, width = tokens.shape
    core = lax.axis_index("inp")
    half = width // 2
    query_cols = query_weight.shape[1]
    key_cols = key_matrix.shape[1]
    normed = rms_normed(tokens, norm_gain)
    own = lax.dynamic_slice_in_dim(normed, core * half, half, 2).reshape(steps * rows, half)
    tag = jnp.stack([positions // 128, positions % 128], axis=-1).astype(jnp.bfloat16)
    tag = jnp.pad(jnp.tile(tag, (steps, 1)), ((0, 0), (0, 126)))
    lower, upper = gather_blocks(jnp.concatenate([own, tag], axis=1))

    def multiply(block):
        return jnp.concatenate(
            [
                jnp.dot(block[:, :half], weight, preferred_element_type=jnp.float32)
                for weight in (query_weight, key_matrix, value_matrix)
            ],
            axis=-1,
        )

    sums = pair_summed(lower, upper, multiply)
    tags = jnp.where(core == 0, jnp.stack([b[:, half : half + 2] for b in lower]), jnp.stack([b[:, half : half + 2] for b in upper]))
    tags = tags.astype(jnp.float32)
    placed = tags[..., 0] * 128.0 + tags[..., 1]
    placed = placed.reshape(4, steps, rows) + jnp.arange(steps, dtype=jnp.float32)[None, :, None]
    placed = placed.reshape(4, steps * rows)
    turned = query_cols + key_cols
    rotated = rotate(sums[..., :turned].reshape(4, steps * rows, -1, HEAD_SIZE), placed)
    outgoing = jnp.concatenate([rotated.reshape(4, steps * rows, turned), sums[..., turned:]], axis=-1).astype(jnp.bfloat16)
    heads = jnp.stack(in_order(hand_out([outgoing[k] for k in range(4)])))
    heads = heads.reshape(4, steps, rows, -1, HEAD_SIZE)
    group = query_cols // HEAD_SIZE
    attended = attend_both(
        heads[:, :, :, :group], heads[:, :, :, group], heads[:, :, :, group + 1], cache_keys, cache_values, lengths
    )
    lower, upper = gather_blocks(attended.reshape(steps * rows, half))
    mixed = pair_summed(
        lower, upper, lambda block: jnp.dot(block, output_weight, preferred_element_type=jnp.float32)
    ).astype(jnp.bfloat16)
    own_half = jnp.concatenate(in_order(hand_out([mixed[k] for k in range(4)])), axis=-1)
    other_half = swap_cores(own_half)
    whole = jnp.concatenate(
        [jnp.where(core == 0, own_half, other_half), jnp.where(core == 0, other_half, own_half)], axis=-1
    )
    return whole.reshape(steps, rows, width)


def body(
    tokens,
    norm_gain,
    query_weight,
    key_matrix,
    value_matrix,
    output_weight,
    cache_keys,
    stored_cache_values,
    lengths,
    positions,
):
    normalized_input = rms_normed(tokens, norm_gain)
    key_list = []
    value_list = []
    results = []
    for token_step in range(2):
        queries, incoming_keys, incoming_values = project(
            normalized_input[token_step : token_step + 1],
            query_weight,
            key_matrix,
            value_matrix,
            positions,
            token_step,
        )
        key_list.append(incoming_keys[0])
        value_list.append(incoming_values[0])
        attended = attend_one(
            queries[0],
            jnp.stack(key_list),
            jnp.stack(value_list),
            cache_keys,
            stored_cache_values,
            lengths,
        )
        results.append(mix_out(attended[None], output_weight)[0])
    return jnp.stack(results)


def solution(mesh):
    placed = (
        P(None, ("group", "out"), None),
        P(),
        P("inp", "out"),
        P("inp", "out"),
        P("inp", "out"),
        P("inp", "out"),
        P(("group", "out"), None, "inp", None),
        P(("group", "out"), None, "inp", None),
        P(("group", "out")),
        P(("group", "out")),
    )
    chosen = eight_chip_body if (mesh.shape["out"], mesh.shape["inp"]) == (8, 2) else body
    return jax.shard_map(
        chosen, mesh=mesh, in_specs=placed, out_specs=P(None, ("group", "out"), None), check_vma=False
    )
```

```python
import math

import jax
import jax.numpy as jnp
from jax import lax
from jax.experimental import pallas as pl
from jax.experimental.pallas import tpu as pltpu
from jax.sharding import PartitionSpec as P

HEAD_SIZE = 128


def rms_normed(tokens, gain):
    values = tokens.astype(jnp.float32)
    factor = lax.rsqrt(jnp.mean(values * values, axis=-1, keepdims=True) + 1e-05)
    return (values * factor * gain).astype(jnp.bfloat16)


def rotate(heads, position):
    head_size = heads.shape[-1]
    half_size = head_size // 2
    frequency = jnp.exp(
        -math.log(500000.0) * 2.0 * jnp.arange(half_size, dtype=jnp.float32) / head_size
    )
    angles = position.astype(jnp.float32)[..., None, None] * frequency
    cosine = jnp.cos(angles)
    sine_part = jnp.sin(angles)
    leading = heads[..., :half_size]
    trailing = heads[..., half_size:]
    return jnp.concatenate(
        [leading * cosine - trailing * sine_part, trailing * cosine + leading * sine_part], axis=-1
    )


def attend_one(queries, new_keys, new_values, cache_keys, stored_cache_values, lengths):
    count_of_rows, head_count, head_size = queries.shape
    key_heads = cache_keys.shape[2]
    grouped = queries.reshape(count_of_rows, key_heads, head_count // key_heads, head_size)
    factor = head_size ** (-0.5)
    cached = (
        jnp.einsum("rkgd,rckd->rkgc", grouped, cache_keys, preferred_element_type=jnp.float32)
        * factor
    )
    visible = jnp.arange(cache_keys.shape[1])[None, :] < lengths[:, None]
    cached = jnp.where(visible[:, None, None, :], cached, -jnp.inf)
    fresh_scores = (
        jnp.einsum("rkgd,nrkd->rkgn", grouped, new_keys, preferred_element_type=jnp.float32)
        * factor
    )
    highest = jnp.maximum(jnp.max(cached, axis=-1), jnp.max(fresh_scores, axis=-1))
    cached_exp = jnp.exp(cached - highest[..., None])
    fresh_exp = jnp.exp(fresh_scores - highest[..., None])
    totals = jnp.sum(cached_exp, axis=-1) + jnp.sum(fresh_exp, axis=-1)
    cached_prob = (cached_exp / totals[..., None]).astype(jnp.bfloat16)
    fresh_prob = (fresh_exp / totals[..., None]).astype(jnp.bfloat16)
    attended = jnp.einsum(
        "rkgc,rckd->rkgd", cached_prob, stored_cache_values, preferred_element_type=jnp.float32
    )
    attended = attended + jnp.einsum(
        "rkgn,nrkd->rkgd", fresh_prob, new_values, preferred_element_type=jnp.float32
    )
    return attended.reshape(count_of_rows, head_count * head_size).astype(jnp.bfloat16)


def project(normalized_input, query_weight, key_matrix, value_matrix, positions, first_step):
    out_count = lax.axis_size("out")
    inp_count = lax.axis_size("inp")
    inp_index = lax.axis_index("inp")
    step_count = normalized_input.shape[0]
    row_local = normalized_input.shape[1]
    feature_width = normalized_input.shape[2] // inp_count
    own_slice = lax.dynamic_slice_in_dim(
        normalized_input, inp_index * feature_width, feature_width, 2
    )
    query_cols = query_weight.shape[1]
    key_cols = key_matrix.shape[1]
    block_width = query_cols + 2 * key_cols
    shard_rows = lax.all_gather(own_slice, "out", axis=1, tiled=True)
    partials = jnp.concatenate(
        [
            jnp.dot(shard_rows, weight, preferred_element_type=jnp.float32)
            for weight in (query_weight, key_matrix, value_matrix)
        ],
        axis=-1,
    )
    totals = lax.psum(partials, "inp")
    regrouped = lax.all_to_all(totals, "out", split_axis=1, concat_axis=2, tiled=True)
    regrouped = regrouped.reshape(step_count, row_local, out_count, block_width)
    block_count = out_count // inp_count
    summed = lax.dynamic_slice_in_dim(regrouped, inp_index * block_count, block_count, 2)
    query_part = summed[..., :query_cols].reshape(step_count, row_local, -1, HEAD_SIZE)
    key_part = summed[..., query_cols : query_cols + key_cols].reshape(
        step_count, row_local, -1, HEAD_SIZE
    )
    value_part = summed[..., query_cols + key_cols :].reshape(step_count, row_local, -1, HEAD_SIZE)
    placed = positions[None, :] + (first_step + jnp.arange(step_count, dtype=jnp.int32))[:, None]
    queries = rotate(query_part, placed).astype(jnp.bfloat16)
    incoming_keys = rotate(key_part, placed).astype(jnp.bfloat16)
    incoming_values = value_part.astype(jnp.bfloat16)
    return (queries, incoming_keys, incoming_values)


def mix_out(attended, output_weight):
    partials = jnp.dot(
        lax.all_gather(attended, "out", axis=1, tiled=True),
        output_weight,
        preferred_element_type=jnp.float32,
    )
    totals = lax.psum(partials, "inp")
    return lax.all_to_all(
        totals.astype(jnp.bfloat16), "out", split_axis=1, concat_axis=2, tiled=True
    )


def exchange_orders(step):
    return {"far": (4, 4), "near": (2, 1), "last": (1, 2)}[step]


def swap_blocks(block, step):
    flips = exchange_orders(step)
    pairs = [(2 * o + i, 2 * (o ^ flips[i]) + i) for o in range(8) for i in range(2)]
    return lax.ppermute(block, ("out", "inp"), pairs)


def gather_blocks(block):
    far = swap_blocks(block, "far")
    near = swap_blocks(block, "near")
    last = swap_blocks(block, "last")
    near_last = swap_blocks(near, "last")
    far_near = swap_blocks(far, "near")
    far_last = swap_blocks(far, "last")
    far_near_last = swap_blocks(far_near, "last")
    return (block, near, last, near_last), (far, far_near, far_last, far_near_last)


def swap_cores(block):
    return lax.ppermute(block, "inp", [(0, 1), (1, 0)])


def offset_of(core, place):
    return (0, 2, 1, 3)[place] if core == 0 else place


def hand_out(blocks):
    received = []
    for place, block in enumerate(blocks):
        pairs = []
        for o in range(8):
            for i in range(2):
                target = o ^ (4 * i) ^ offset_of(i, place)
                pairs.append((2 * o + i, 2 * target + o // 4))
        received.append(lax.ppermute(block, ("out", "inp"), pairs))
    return received


def place_of(column, crossed):
    offset = column ^ (lax.axis_index("out") % 4)
    swapped = jnp.where((offset == 1) | (offset == 2), 3 - offset, offset)
    return jnp.where(crossed == 0, swapped, offset)


def crossing(core):
    return (lax.axis_index("out") // 4) ^ core


def in_order(received):
    crossed = crossing(lax.axis_index("inp"))
    stacked = jnp.stack(received)
    return jnp.stack([lax.dynamic_index_in_dim(stacked, place_of(c, crossed), 0, keepdims=False) for c in range(4)])


VMEM_SPEC = pl.BlockSpec(memory_space=pltpu.VMEM)
SMEM_SPEC = pl.BlockSpec(memory_space=pltpu.SMEM)
MEGABYTE = 1 << 20


def on_chip(kernel, out_shape, scalars, *operands, scratch=(), megabytes=16, moved=1, place=VMEM_SPEC):
    return pl.pallas_call(
        kernel,
        out_shape=out_shape,
        in_specs=[SMEM_SPEC] * len(scalars) + [place] * len(operands),
        out_specs=jax.tree.map(lambda _: VMEM_SPEC, out_shape),
        scratch_shapes=scratch,
        compiler_params=pltpu.CompilerParams(vmem_limit_bytes=megabytes * MEGABYTE),
        cost_estimate=pl.CostEstimate(flops=0, bytes_accessed=moved * MEGABYTE, transcendentals=0),
    )(*scalars, *operands)


def norm_kernel(position_hbm, token_hbm, gain_hbm, out_ref, position_ref, token_ref, gain_ref, arrivals):
    pairs = ((token_hbm, token_ref), (gain_hbm, gain_ref), (position_hbm, position_ref))
    copies = [pltpu.make_async_copy(source, target, arrivals.at[n]) for n, (source, target) in enumerate(pairs)]
    for copy in copies:
        copy.start()
    core = lax.axis_index("inp")
    half = token_ref.shape[1] // 2
    rows = position_ref.shape[0]
    own = pl.ds(pl.multiple_of(core * half, 128), half)
    copies[0].wait()
    values = token_ref[...].astype(jnp.float32)
    factor = lax.rsqrt(jnp.mean(values * values, axis=-1, keepdims=True) + 1e-05)
    copies[1].wait()
    out_ref[:, :half] = (token_ref[:, own].astype(jnp.float32) * factor * gain_ref[:, own]).astype(jnp.bfloat16)
    shape = (token_ref.shape[0], 128)
    row = lax.broadcasted_iota(jnp.int32, shape, 0) % rows
    lane = lax.broadcasted_iota(jnp.int32, shape, 1)
    tag = jnp.zeros(shape, jnp.int32)
    copies[2].wait()
    for r in range(rows):
        place = position_ref[r]
        tag = jnp.where(row == r, jnp.where(lane == 0, place // 128, place % 128), tag)
    out_ref[:, half:] = tag.astype(jnp.float32).astype(jnp.bfloat16)


def fetch_kernel(*refs):
    count = (len(refs) - 1) // 2
    arrivals = refs[-1]
    copies = []
    for n in range(count):
        source, target = refs[n], refs[count + n]
        size = source.shape[0] // 4
        for part in range(4):
            here = pl.ds(part * size, size)
            copies.append(pltpu.make_async_copy(source.at[here], target.at[here], arrivals.at[n, part]))
    for copy in copies:
        copy.start()
    for copy in copies:
        copy.wait()


def distant(array):
    return pltpu.with_memory_space_constraint(array, pltpu.HBM)


def fetched(*arrays):
    return pl.pallas_call(
        fetch_kernel,
        out_shape=[pltpu.VMEM(array.shape, array.dtype) for array in arrays],
        in_specs=[pl.BlockSpec(memory_space=pl.ANY)] * len(arrays),
        out_specs=[VMEM_SPEC] * len(arrays),
        scratch_shapes=[pltpu.SemaphoreType.DMA((len(arrays), 4))],
        compiler_params=pltpu.CompilerParams(vmem_limit_bytes=MEGABYTE),
        cost_estimate=pl.CostEstimate(
            flops=0,
            bytes_accessed=sum(array.size * array.dtype.itemsize for array in arrays),
            transcendentals=0,
        ),
    )(*map(distant, arrays))


def stack_rows(core, pieces, rows_ref):
    rows, depth = pieces[0].shape[0], rows_ref.shape[1]
    for n, piece in enumerate(pieces):
        upper = n // 4
        half = (upper + core + 1) % 2
        start = pl.multiple_of((half * 4 + n % 4) * rows, rows)
        rows_ref[pl.ds(start, rows), :] = piece[:, :depth]


def project_kernel(*refs):
    core = lax.axis_index("inp")
    pieces, (query_ref, key_ref, value_ref, given_ref, kept_ref, tag_ref, rows_ref) = refs[:8], refs[8:]
    stack_rows(core, pieces, rows_ref)
    count = given_ref.shape[0]
    rows, depth = pieces[0].shape[0], rows_ref.shape[1]
    for n in range(4):
        lower, upper = pieces[n][:, depth:], pieces[n + 4][:, depth:]
        tag_ref[pl.ds(n * rows, rows), :] = jnp.where(core == 0, lower.astype(jnp.float32), upper.astype(jnp.float32))
    first = 0
    for weight_ref in (query_ref, key_ref, value_ref):
        width = weight_ref.shape[1]
        block = min(256, width)
        for at in range(0, width, block):
            sums = jnp.dot(rows_ref[...], weight_ref[:, at : at + block], preferred_element_type=jnp.float32)
            given_ref[:, first + at : first + at + block] = sums[:count]
            kept_ref[:, first + at : first + at + block] = sums[count:]
        first += width


def mix_kernel(*refs):
    core = lax.axis_index("inp")
    pieces, (weight_ref, given_ref, kept_ref, rows_ref) = refs[:8], refs[8:]
    stack_rows(core, pieces, rows_ref)
    count = given_ref.shape[0]
    for at in range(0, weight_ref.shape[1], 256):
        sums = jnp.dot(rows_ref[...], weight_ref[:, at : at + 256], preferred_element_type=jnp.float32)
        given_ref[:, at : at + 256] = sums[:count]
        kept_ref[:, at : at + 256] = sums[count:]


ARRIVAL = (0, 2, 1, 3)


def turn_kernel(kept_ref, arrived_ref, cosine_ref, sine_ref, *out_refs):
    rows = out_refs[0].shape[0]
    heads = kept_ref.shape[1] // HEAD_SIZE
    for n, out_ref in enumerate(out_refs):
        here = pl.ds(n * rows, rows)
        there = pl.ds(ARRIVAL[n] * rows, rows)
        cosine, sine = cosine_ref[here, :], sine_ref[here, :]
        for head in range(heads):
            columns = slice(head * HEAD_SIZE, (head + 1) * HEAD_SIZE)
            total = kept_ref[here, columns] + arrived_ref[there, columns]
            if head < heads - 1:
                total = total * cosine + pltpu.roll(total, HEAD_SIZE // 2, 1) * sine
            out_ref[:, columns] = total.astype(jnp.bfloat16)


def round_kernel(kept_ref, arrived_ref, *out_refs):
    rows = out_refs[0].shape[0]
    for n, out_ref in enumerate(out_refs):
        total = kept_ref[pl.ds(n * rows, rows), :] + arrived_ref[pl.ds(ARRIVAL[n] * rows, rows), :]
        out_ref[...] = total.astype(jnp.bfloat16)


def place_kernel(own_places, other_places, own_ref, other_ref, out_ref):
    core = lax.axis_index("inp")
    width = own_ref.shape[2]
    for column in range(4):
        own = own_ref[own_places[column]]
        other = other_ref[other_places[column]]
        left = jnp.where(core == 0, own.astype(jnp.float32), other.astype(jnp.float32))
        right = jnp.where(core == 0, other.astype(jnp.float32), own.astype(jnp.float32))
        out_ref[:, column * width : (column + 1) * width] = left.astype(jnp.bfloat16)
        out_ref[:, (column + 4) * width : (column + 5) * width] = right.astype(jnp.bfloat16)


def attend_both(queries, new_keys, new_values, cache_keys, cache_values, lengths):
    factor = HEAD_SIZE ** (-0.5)
    steps = queries.shape[1]
    cached = jnp.einsum("ktrgd,rckd->rktgc", queries, cache_keys, preferred_element_type=jnp.float32) * factor
    visible = jnp.arange(cache_keys.shape[1])[None, :] < lengths[:, None]
    cached = jnp.where(visible[:, None, None, None, :], cached, -jnp.inf)
    fresh = jnp.einsum("ktrgd,knrd->rktgn", queries, new_keys, preferred_element_type=jnp.float32) * factor
    causal = jnp.arange(steps)[:, None] >= jnp.arange(steps)[None, :]
    fresh = jnp.where(causal[None, None, :, None, :], fresh, -jnp.inf)
    highest = jnp.maximum(jnp.max(cached, axis=-1), jnp.max(fresh, axis=-1))
    cached_exp = jnp.exp(cached - highest[..., None])
    fresh_exp = jnp.exp(fresh - highest[..., None])
    totals = jnp.sum(cached_exp, axis=-1) + jnp.sum(fresh_exp, axis=-1)
    cached_prob = (cached_exp / totals[..., None]).astype(jnp.bfloat16)
    fresh_prob = (fresh_exp / totals[..., None]).astype(jnp.bfloat16)
    attended = jnp.einsum("rktgc,rckd->trkgd", cached_prob, cache_values, preferred_element_type=jnp.float32)
    attended = attended + jnp.einsum("rktgn,knrd->trkgd", fresh_prob, new_values, preferred_element_type=jnp.float32)
    return attended.astype(jnp.bfloat16)


def resident(array):
    return pltpu.with_memory_space_constraint(array, pltpu.VMEM)


def eight_chip_body(
    tokens, norm_gain, query_weight, key_matrix, value_matrix, output_weight, cache_keys, cache_values, lengths, positions
):
    steps, rows, width = tokens.shape
    count = steps * rows
    half = width // 2
    core = lax.axis_index("inp")
    query_cols = query_weight.shape[1]
    qkv_cols = query_cols + 2 * key_matrix.shape[1]
    shape = jax.ShapeDtypeStruct
    own = on_chip(
        norm_kernel,
        shape((count, half + 128), jnp.bfloat16),
        (),
        distant(positions),
        distant(tokens.reshape(count, width)),
        distant(norm_gain.reshape(1, width)),
        scratch=[
            pltpu.SMEM((rows,), jnp.int32),
            pltpu.VMEM((count, width), jnp.bfloat16),
            pltpu.VMEM((1, width), jnp.float32),
            pltpu.SemaphoreType.DMA((3,)),
        ],
        place=pl.BlockSpec(memory_space=pltpu.HBM),
    )
    near_query, near_key, near_value = fetched(query_weight, key_matrix, value_matrix)
    cache_keys, cache_values = fetched(cache_keys, cache_values)
    lower, upper = gather_blocks(own)
    given, kept, tags = on_chip(
        project_kernel,
        [shape((4 * count, qkv_cols), jnp.float32)] * 2 + [shape((4 * count, 128), jnp.float32)],
        (),
        *lower,
        *upper,
        resident(near_query),
        resident(near_key),
        resident(near_value),
        scratch=[pltpu.VMEM((8 * count, half), jnp.bfloat16)],
    )
    arrived = swap_cores(given)
    frequency = jnp.exp(
        -math.log(500000.0) * 2.0 * jnp.arange(HEAD_SIZE // 2, dtype=jnp.float32) / HEAD_SIZE
    )
    step = (jnp.arange(4 * count) // rows % steps).astype(jnp.float32)
    angles = (tags[:, 0] * 128.0 + tags[:, 1] + step)[:, None] * frequency
    cosine, sine = jnp.cos(angles), jnp.sin(angles)
    outgoing = on_chip(
        turn_kernel,
        [shape((count, qkv_cols), jnp.bfloat16)] * 4,
        (),
        kept,
        arrived,
        jnp.concatenate([cosine, cosine], axis=-1),
        jnp.concatenate([-sine, sine], axis=-1),
    )
    heads = in_order(hand_out(outgoing)).reshape(4, steps, rows, -1, HEAD_SIZE)
    group = query_cols // HEAD_SIZE
    attended = attend_both(
        heads[:, :, :, :group], heads[:, :, :, group], heads[:, :, :, group + 1], cache_keys, cache_values, lengths
    )
    lower, upper = gather_blocks(attended.reshape(count, half))
    mix_cols = output_weight.shape[1]
    given, kept = on_chip(
        mix_kernel,
        [shape((4 * count, mix_cols), jnp.float32)] * 2,
        (),
        *lower,
        *upper,
        resident(output_weight),
        scratch=[pltpu.VMEM((8 * count, half), jnp.bfloat16)],
    )
    outgoing = on_chip(
        round_kernel, [shape((count, mix_cols), jnp.bfloat16)] * 4, (), kept, swap_cores(given)
    )
    own_half = jnp.stack(hand_out(outgoing))
    own_places = jnp.stack([place_of(c, crossing(core)) for c in range(4)]).astype(jnp.int32)
    other_places = jnp.stack([place_of(c, crossing(1 - core)) for c in range(4)]).astype(jnp.int32)
    mixed = on_chip(
        place_kernel,
        shape((count, width), jnp.bfloat16),
        (own_places, other_places),
        own_half,
        swap_cores(own_half),
    )
    return mixed.reshape(steps, rows, width)


def body(
    tokens,
    norm_gain,
    query_weight,
    key_matrix,
    value_matrix,
    output_weight,
    cache_keys,
    stored_cache_values,
    lengths,
    positions,
):
    normalized_input = rms_normed(tokens, norm_gain)
    key_list = []
    value_list = []
    results = []
    for token_step in range(2):
        queries, incoming_keys, incoming_values = project(
            normalized_input[token_step : token_step + 1],
            query_weight,
            key_matrix,
            value_matrix,
            positions,
            token_step,
        )
        key_list.append(incoming_keys[0])
        value_list.append(incoming_values[0])
        attended = attend_one(
            queries[0],
            jnp.stack(key_list),
            jnp.stack(value_list),
            cache_keys,
            stored_cache_values,
            lengths,
        )
        results.append(mix_out(attended[None], output_weight)[0])
    return jnp.stack(results)


def solution(mesh):
    placed = (
        P(None, ("group", "out"), None),
        P(),
        P("inp", "out"),
        P("inp", "out"),
        P("inp", "out"),
        P("inp", "out"),
        P(("group", "out"), None, "inp", None),
        P(("group", "out"), None, "inp", None),
        P(("group", "out")),
        P(("group", "out")),
    )
    chosen = eight_chip_body if (mesh.shape["out"], mesh.shape["inp"]) == (8, 2) else body
    return jax.shard_map(
        chosen, mesh=mesh, in_specs=placed, out_specs=P(None, ("group", "out"), None), check_vma=False
    )
```

```python
import math

import jax
import jax.numpy as jnp
from jax import lax
from jax.experimental import pallas as pl
from jax.experimental.pallas import tpu as pltpu
from jax.sharding import PartitionSpec as P

HEAD_SIZE = 128


def rms_normed(tokens, gain):
    values = tokens.astype(jnp.float32)
    factor = lax.rsqrt(jnp.mean(values * values, axis=-1, keepdims=True) + 1e-05)
    return (values * factor * gain).astype(jnp.bfloat16)


def rotate(heads, position):
    head_size = heads.shape[-1]
    half_size = head_size // 2
    frequency = jnp.exp(
        -math.log(500000.0) * 2.0 * jnp.arange(half_size, dtype=jnp.float32) / head_size
    )
    angles = position.astype(jnp.float32)[..., None, None] * frequency
    cosine = jnp.cos(angles)
    sine_part = jnp.sin(angles)
    leading = heads[..., :half_size]
    trailing = heads[..., half_size:]
    return jnp.concatenate(
        [leading * cosine - trailing * sine_part, trailing * cosine + leading * sine_part], axis=-1
    )


def attend_one(queries, new_keys, new_values, cache_keys, stored_cache_values, lengths):
    count_of_rows, head_count, head_size = queries.shape
    key_heads = cache_keys.shape[2]
    grouped = queries.reshape(count_of_rows, key_heads, head_count // key_heads, head_size)
    factor = head_size ** (-0.5)
    cached = (
        jnp.einsum("rkgd,rckd->rkgc", grouped, cache_keys, preferred_element_type=jnp.float32)
        * factor
    )
    visible = jnp.arange(cache_keys.shape[1])[None, :] < lengths[:, None]
    cached = jnp.where(visible[:, None, None, :], cached, -jnp.inf)
    fresh_scores = (
        jnp.einsum("rkgd,nrkd->rkgn", grouped, new_keys, preferred_element_type=jnp.float32)
        * factor
    )
    highest = jnp.maximum(jnp.max(cached, axis=-1), jnp.max(fresh_scores, axis=-1))
    cached_exp = jnp.exp(cached - highest[..., None])
    fresh_exp = jnp.exp(fresh_scores - highest[..., None])
    totals = jnp.sum(cached_exp, axis=-1) + jnp.sum(fresh_exp, axis=-1)
    cached_prob = (cached_exp / totals[..., None]).astype(jnp.bfloat16)
    fresh_prob = (fresh_exp / totals[..., None]).astype(jnp.bfloat16)
    attended = jnp.einsum(
        "rkgc,rckd->rkgd", cached_prob, stored_cache_values, preferred_element_type=jnp.float32
    )
    attended = attended + jnp.einsum(
        "rkgn,nrkd->rkgd", fresh_prob, new_values, preferred_element_type=jnp.float32
    )
    return attended.reshape(count_of_rows, head_count * head_size).astype(jnp.bfloat16)


def project(normalized_input, query_weight, key_matrix, value_matrix, positions, first_step):
    out_count = lax.axis_size("out")
    inp_count = lax.axis_size("inp")
    inp_index = lax.axis_index("inp")
    step_count = normalized_input.shape[0]
    row_local = normalized_input.shape[1]
    feature_width = normalized_input.shape[2] // inp_count
    own_slice = lax.dynamic_slice_in_dim(
        normalized_input, inp_index * feature_width, feature_width, 2
    )
    query_cols = query_weight.shape[1]
    key_cols = key_matrix.shape[1]
    block_width = query_cols + 2 * key_cols
    shard_rows = lax.all_gather(own_slice, "out", axis=1, tiled=True)
    partials = jnp.concatenate(
        [
            jnp.dot(shard_rows, weight, preferred_element_type=jnp.float32)
            for weight in (query_weight, key_matrix, value_matrix)
        ],
        axis=-1,
    )
    totals = lax.psum(partials, "inp")
    regrouped = lax.all_to_all(totals, "out", split_axis=1, concat_axis=2, tiled=True)
    regrouped = regrouped.reshape(step_count, row_local, out_count, block_width)
    block_count = out_count // inp_count
    summed = lax.dynamic_slice_in_dim(regrouped, inp_index * block_count, block_count, 2)
    query_part = summed[..., :query_cols].reshape(step_count, row_local, -1, HEAD_SIZE)
    key_part = summed[..., query_cols : query_cols + key_cols].reshape(
        step_count, row_local, -1, HEAD_SIZE
    )
    value_part = summed[..., query_cols + key_cols :].reshape(step_count, row_local, -1, HEAD_SIZE)
    placed = positions[None, :] + (first_step + jnp.arange(step_count, dtype=jnp.int32))[:, None]
    queries = rotate(query_part, placed).astype(jnp.bfloat16)
    incoming_keys = rotate(key_part, placed).astype(jnp.bfloat16)
    incoming_values = value_part.astype(jnp.bfloat16)
    return (queries, incoming_keys, incoming_values)


def mix_out(attended, output_weight):
    partials = jnp.dot(
        lax.all_gather(attended, "out", axis=1, tiled=True),
        output_weight,
        preferred_element_type=jnp.float32,
    )
    totals = lax.psum(partials, "inp")
    return lax.all_to_all(
        totals.astype(jnp.bfloat16), "out", split_axis=1, concat_axis=2, tiled=True
    )


def exchange_orders(step):
    return {"far": (4, 4), "near": (2, 1), "last": (1, 2)}[step]


def swap_blocks(block, step):
    flips = exchange_orders(step)
    pairs = [(2 * o + i, 2 * (o ^ flips[i]) + i) for o in range(8) for i in range(2)]
    return lax.ppermute(block, ("out", "inp"), pairs)


def gather_blocks(block, *marks):
    far = swap_blocks(block, "far")
    near = swap_blocks(block, "near")
    last = swap_blocks(block, "last")
    if marks:
        far = after(far, *marks)
    near_last = swap_blocks(near, "last")
    far_near = swap_blocks(far, "near")
    far_last = swap_blocks(far, "last")
    far_near_last = swap_blocks(far_near, "last")
    return (block, near, last, near_last), (far, far_near, far_last, far_near_last)


def swap_cores(block):
    return lax.ppermute(block, "inp", [(0, 1), (1, 0)])


def offset_of(core, place):
    return (0, 2, 1, 3)[place] if core == 0 else place


def hand_out(blocks):
    received = []
    for place, block in enumerate(blocks):
        pairs = []
        for o in range(8):
            for i in range(2):
                target = o ^ (4 * i) ^ offset_of(i, place)
                pairs.append((2 * o + i, 2 * target + o // 4))
        received.append(lax.ppermute(block, ("out", "inp"), pairs))
    return received


def place_of(column, crossed):
    offset = column ^ (lax.axis_index("out") % 4)
    swapped = jnp.where((offset == 1) | (offset == 2), 3 - offset, offset)
    return jnp.where(crossed == 0, swapped, offset)


def crossing(core):
    return (lax.axis_index("out") // 4) ^ core


def in_order(received):
    crossed = crossing(lax.axis_index("inp"))
    stacked = jnp.stack(received)
    return jnp.stack([lax.dynamic_index_in_dim(stacked, place_of(c, crossed), 0, keepdims=False) for c in range(4)])


VMEM_SPEC = pl.BlockSpec(memory_space=pltpu.VMEM)
SMEM_SPEC = pl.BlockSpec(memory_space=pltpu.SMEM)
MEGABYTE = 1 << 20


def on_chip(kernel, out_shape, scalars, *operands, scratch=(), megabytes=8, moved=1, place=VMEM_SPEC):
    return pl.pallas_call(
        kernel,
        out_shape=out_shape,
        in_specs=[SMEM_SPEC] * len(scalars) + [place] * len(operands),
        out_specs=jax.tree.map(lambda _: VMEM_SPEC, out_shape),
        scratch_shapes=scratch,
        compiler_params=pltpu.CompilerParams(vmem_limit_bytes=megabytes * MEGABYTE),
        cost_estimate=pl.CostEstimate(flops=0, bytes_accessed=moved * MEGABYTE, transcendentals=0),
    )(*scalars, *operands)


def norm_kernel(position_hbm, token_hbm, gain_hbm, out_ref, position_ref, token_ref, gain_ref, arrivals):
    pairs = ((token_hbm, token_ref), (gain_hbm, gain_ref), (position_hbm, position_ref))
    copies = [pltpu.make_async_copy(source, target, arrivals.at[n]) for n, (source, target) in enumerate(pairs)]
    for copy in copies:
        copy.start()
    core = lax.axis_index("inp")
    half = token_ref.shape[1] // 2
    rows = position_ref.shape[0]
    own = pl.ds(pl.multiple_of(core * half, 128), half)
    copies[0].wait()
    values = token_ref[...].astype(jnp.float32)
    factor = lax.rsqrt(jnp.mean(values * values, axis=-1, keepdims=True) + 1e-05)
    copies[1].wait()
    out_ref[:, :half] = (token_ref[:, own].astype(jnp.float32) * factor * gain_ref[:, own]).astype(jnp.bfloat16)
    shape = (token_ref.shape[0], 128)
    row = lax.broadcasted_iota(jnp.int32, shape, 0) % rows
    lane = lax.broadcasted_iota(jnp.int32, shape, 1)
    tag = jnp.zeros(shape, jnp.int32)
    copies[2].wait()
    for r in range(rows):
        place = position_ref[r]
        tag = jnp.where(row == r, jnp.where(lane == 0, place // 128, place % 128), tag)
    out_ref[:, half:] = tag.astype(jnp.float32).astype(jnp.bfloat16)


def fetch_kernel(*refs):
    count = (len(refs) - 2) // 2
    mark_ref, arrivals = refs[-2:]
    copies = []
    for n in range(count):
        source, target = refs[n], refs[count + n]
        size = source.shape[0] // 4
        for part in range(4):
            here = pl.ds(part * size, size)
            copies.append(pltpu.make_async_copy(source.at[here], target.at[here], arrivals.at[n, part]))
    for copy in copies:
        copy.start()
    mark_ref[...] = jnp.zeros_like(mark_ref)
    for copy in copies:
        copy.wait()


def distant(array):
    return pltpu.with_memory_space_constraint(array, pltpu.HBM)


ANYWHERE = pl.BlockSpec(memory_space=pl.ANY)


def fetched(*arrays):
    *near, mark = pl.pallas_call(
        fetch_kernel,
        out_shape=[pltpu.VMEM(array.shape, array.dtype) for array in arrays]
        + [jax.ShapeDtypeStruct((8, 128), jnp.float32)],
        in_specs=[ANYWHERE] * len(arrays),
        out_specs=[VMEM_SPEC] * (len(arrays) + 1),
        scratch_shapes=[pltpu.SemaphoreType.DMA((len(arrays), 4))],
        compiler_params=pltpu.CompilerParams(vmem_limit_bytes=MEGABYTE),
        cost_estimate=pl.CostEstimate(
            flops=0,
            bytes_accessed=sum(array.size * array.dtype.itemsize for array in arrays),
            transcendentals=0,
        ),
    )(*map(distant, arrays))
    return near, mark


def after_kernel(*refs):
    pass


def after(block, *others):
    return pl.pallas_call(
        after_kernel,
        out_shape=jax.ShapeDtypeStruct(block.shape, block.dtype),
        in_specs=[ANYWHERE] * (1 + len(others)),
        out_specs=ANYWHERE,
        input_output_aliases={0: 0},
        compiler_params=pltpu.CompilerParams(vmem_limit_bytes=MEGABYTE),
    )(block, *others)


def stack_rows(core, pieces, rows_ref):
    rows, depth = pieces[0].shape[0], rows_ref.shape[1]
    for n, piece in enumerate(pieces):
        upper = n // 4
        half = (upper + core + 1) % 2
        start = pl.multiple_of((half * 4 + n % 4) * rows, rows)
        rows_ref[pl.ds(start, rows), :] = piece[:, :depth]


def project_kernel(*refs):
    core = lax.axis_index("inp")
    pieces, (query_ref, key_ref, value_ref, given_ref, kept_ref, tag_ref, rows_ref) = refs[:8], refs[8:]
    stack_rows(core, pieces, rows_ref)
    count = given_ref.shape[0]
    rows, depth = pieces[0].shape[0], rows_ref.shape[1]
    for n in range(4):
        lower, upper = pieces[n][:, depth:], pieces[n + 4][:, depth:]
        tag_ref[pl.ds(n * rows, rows), :] = jnp.where(core == 0, lower.astype(jnp.float32), upper.astype(jnp.float32))
    first = 0
    for weight_ref in (query_ref, key_ref, value_ref):
        width = weight_ref.shape[1]
        block = min(256, width)
        for at in range(0, width, block):
            sums = jnp.dot(rows_ref[...], weight_ref[:, at : at + block], preferred_element_type=jnp.float32)
            given_ref[:, first + at : first + at + block] = sums[:count]
            kept_ref[:, first + at : first + at + block] = sums[count:]
        first += width


def mix_kernel(*refs):
    core = lax.axis_index("inp")
    pieces, (weight_ref, given_ref, kept_ref, rows_ref) = refs[:8], refs[8:]
    stack_rows(core, pieces, rows_ref)
    count = given_ref.shape[0]
    for at in range(0, weight_ref.shape[1], 256):
        sums = jnp.dot(rows_ref[...], weight_ref[:, at : at + 256], preferred_element_type=jnp.float32)
        given_ref[:, at : at + 256] = sums[:count]
        kept_ref[:, at : at + 256] = sums[count:]


ARRIVAL = (0, 2, 1, 3)


def turn_kernel(kept_ref, arrived_ref, cosine_ref, sine_ref, *out_refs):
    rows = out_refs[0].shape[0]
    heads = kept_ref.shape[1] // HEAD_SIZE
    for n, out_ref in enumerate(out_refs):
        here = pl.ds(n * rows, rows)
        there = pl.ds(ARRIVAL[n] * rows, rows)
        cosine, sine = cosine_ref[here, :], sine_ref[here, :]
        for head in range(heads):
            columns = slice(head * HEAD_SIZE, (head + 1) * HEAD_SIZE)
            total = kept_ref[here, columns] + arrived_ref[there, columns]
            if head < heads - 1:
                total = total * cosine + pltpu.roll(total, HEAD_SIZE // 2, 1) * sine
            out_ref[:, columns] = total.astype(jnp.bfloat16)


def round_kernel(kept_ref, arrived_ref, *out_refs):
    rows = out_refs[0].shape[0]
    for n, out_ref in enumerate(out_refs):
        total = kept_ref[pl.ds(n * rows, rows), :] + arrived_ref[pl.ds(ARRIVAL[n] * rows, rows), :]
        out_ref[...] = total.astype(jnp.bfloat16)


def place_kernel(own_ref, other_ref, out_ref):
    core = lax.axis_index("inp")
    width = own_ref.shape[2]
    for column in range(4):
        for ref, its_core in ((own_ref, core), (other_ref, 1 - core)):
            start = pl.multiple_of((its_core * 4 + column) * width, width)
            out_ref[:, pl.ds(start, width)] = ref[place_of(column, crossing(its_core))]


def attend_both(queries, new_keys, new_values, cache_keys, cache_values, lengths):
    factor = HEAD_SIZE ** (-0.5)
    steps = queries.shape[1]
    cached = jnp.einsum("ktrgd,rckd->rktgc", queries, cache_keys, preferred_element_type=jnp.float32) * factor
    visible = jnp.arange(cache_keys.shape[1])[None, :] < lengths[:, None]
    cached = jnp.where(visible[:, None, None, None, :], cached, -jnp.inf)
    fresh = jnp.einsum("ktrgd,knrd->rktgn", queries, new_keys, preferred_element_type=jnp.float32) * factor
    causal = jnp.arange(steps)[:, None] >= jnp.arange(steps)[None, :]
    fresh = jnp.where(causal[None, None, :, None, :], fresh, -jnp.inf)
    highest = jnp.maximum(jnp.max(cached, axis=-1), jnp.max(fresh, axis=-1))
    cached_exp = jnp.exp(cached - highest[..., None])
    fresh_exp = jnp.exp(fresh - highest[..., None])
    totals = jnp.sum(cached_exp, axis=-1) + jnp.sum(fresh_exp, axis=-1)
    cached_prob = (cached_exp / totals[..., None]).astype(jnp.bfloat16)
    fresh_prob = (fresh_exp / totals[..., None]).astype(jnp.bfloat16)
    attended = jnp.einsum("rktgc,rckd->trkgd", cached_prob, cache_values, preferred_element_type=jnp.float32)
    attended = attended + jnp.einsum("rktgn,knrd->trkgd", fresh_prob, new_values, preferred_element_type=jnp.float32)
    return attended.astype(jnp.bfloat16)


def resident(array):
    return pltpu.with_memory_space_constraint(array, pltpu.VMEM)


def eight_chip_body(
    tokens, norm_gain, query_weight, key_matrix, value_matrix, output_weight, cache_keys, cache_values, lengths, positions
):
    steps, rows, width = tokens.shape
    count = steps * rows
    half = width // 2
    core = lax.axis_index("inp")
    query_cols = query_weight.shape[1]
    qkv_cols = query_cols + 2 * key_matrix.shape[1]
    shape = jax.ShapeDtypeStruct
    own = on_chip(
        norm_kernel,
        shape((count, half + 128), jnp.bfloat16),
        (),
        distant(positions),
        distant(tokens.reshape(count, width)),
        distant(norm_gain.reshape(1, width)),
        scratch=[
            pltpu.SMEM((rows,), jnp.int32),
            pltpu.VMEM((count, width), jnp.bfloat16),
            pltpu.VMEM((1, width), jnp.float32),
            pltpu.SemaphoreType.DMA((3,)),
        ],
        place=pl.BlockSpec(memory_space=pltpu.HBM),
    )
    (near_query, near_key, near_value), weight_mark = fetched(query_weight, key_matrix, value_matrix)
    (cache_keys, cache_values), cache_mark = fetched(cache_keys, cache_values)
    lower, upper = gather_blocks(own, weight_mark)
    given, kept, tags = on_chip(
        project_kernel,
        [shape((4 * count, qkv_cols), jnp.float32)] * 2 + [shape((4 * count, 128), jnp.float32)],
        (),
        *lower,
        *upper,
        resident(near_query),
        resident(near_key),
        resident(near_value),
        scratch=[pltpu.VMEM((8 * count, half), jnp.bfloat16)],
    )
    arrived = swap_cores(given)
    frequency = jnp.exp(
        -math.log(500000.0) * 2.0 * jnp.arange(HEAD_SIZE // 2, dtype=jnp.float32) / HEAD_SIZE
    )
    step = (jnp.arange(4 * count) // rows % steps).astype(jnp.float32)
    angles = (tags[:, 0] * 128.0 + tags[:, 1] + step)[:, None] * frequency
    cosine, sine = jnp.cos(angles), jnp.sin(angles)
    outgoing = on_chip(
        turn_kernel,
        [shape((count, qkv_cols), jnp.bfloat16)] * 4,
        (),
        kept,
        arrived,
        jnp.concatenate([cosine, cosine], axis=-1),
        jnp.concatenate([-sine, sine], axis=-1),
    )
    heads = in_order(hand_out(outgoing)).reshape(4, steps, rows, -1, HEAD_SIZE)
    group = query_cols // HEAD_SIZE
    attended = attend_both(
        heads[:, :, :, :group], heads[:, :, :, group], heads[:, :, :, group + 1], cache_keys, cache_values, lengths
    )
    lower, upper = gather_blocks(attended.reshape(count, half))
    mix_cols = output_weight.shape[1]
    given, kept = on_chip(
        mix_kernel,
        [shape((4 * count, mix_cols), jnp.float32)] * 2,
        (),
        *lower,
        *upper,
        resident(output_weight),
        scratch=[pltpu.VMEM((8 * count, half), jnp.bfloat16)],
    )
    outgoing = on_chip(
        round_kernel, [shape((count, mix_cols), jnp.bfloat16)] * 4, (), kept, swap_cores(given)
    )
    own_half = jnp.stack(hand_out(outgoing))
    mixed = on_chip(
        place_kernel,
        shape((count, width), jnp.bfloat16),
        (),
        own_half,
        swap_cores(own_half),
    )
    return mixed.reshape(steps, rows, width)


def body(
    tokens,
    norm_gain,
    query_weight,
    key_matrix,
    value_matrix,
    output_weight,
    cache_keys,
    stored_cache_values,
    lengths,
    positions,
):
    normalized_input = rms_normed(tokens, norm_gain)
    key_list = []
    value_list = []
    results = []
    for token_step in range(2):
        queries, incoming_keys, incoming_values = project(
            normalized_input[token_step : token_step + 1],
            query_weight,
            key_matrix,
            value_matrix,
            positions,
            token_step,
        )
        key_list.append(incoming_keys[0])
        value_list.append(incoming_values[0])
        attended = attend_one(
            queries[0],
            jnp.stack(key_list),
            jnp.stack(value_list),
            cache_keys,
            stored_cache_values,
            lengths,
        )
        results.append(mix_out(attended[None], output_weight)[0])
    return jnp.stack(results)


def solution(mesh):
    placed = (
        P(None, ("group", "out"), None),
        P(),
        P("inp", "out"),
        P("inp", "out"),
        P("inp", "out"),
        P("inp", "out"),
        P(("group", "out"), None, "inp", None),
        P(("group", "out"), None, "inp", None),
        P(("group", "out")),
        P(("group", "out")),
    )
    chosen = eight_chip_body if (mesh.shape["out"], mesh.shape["inp"]) == (8, 2) else body
    return jax.shard_map(
        chosen, mesh=mesh, in_specs=placed, out_specs=P(None, ("group", "out"), None), check_vma=False
    )
```

```python
import math

import jax
import jax.numpy as jnp
from jax import lax
from jax.experimental import pallas as pl
from jax.experimental.pallas import tpu as pltpu
from jax.sharding import PartitionSpec as P

HEAD_SIZE = 128


def rms_normed(tokens, gain):
    values = tokens.astype(jnp.float32)
    factor = lax.rsqrt(jnp.mean(values * values, axis=-1, keepdims=True) + 1e-05)
    return (values * factor * gain).astype(jnp.bfloat16)


def rotate(heads, position):
    head_size = heads.shape[-1]
    half_size = head_size // 2
    frequency = jnp.exp(
        -math.log(500000.0) * 2.0 * jnp.arange(half_size, dtype=jnp.float32) / head_size
    )
    angles = position.astype(jnp.float32)[..., None, None] * frequency
    cosine = jnp.cos(angles)
    sine_part = jnp.sin(angles)
    leading = heads[..., :half_size]
    trailing = heads[..., half_size:]
    return jnp.concatenate(
        [leading * cosine - trailing * sine_part, trailing * cosine + leading * sine_part], axis=-1
    )


def attend_one(queries, new_keys, new_values, cache_keys, stored_cache_values, lengths):
    count_of_rows, head_count, head_size = queries.shape
    key_heads = cache_keys.shape[2]
    grouped = queries.reshape(count_of_rows, key_heads, head_count // key_heads, head_size)
    factor = head_size ** (-0.5)
    cached = (
        jnp.einsum("rkgd,rckd->rkgc", grouped, cache_keys, preferred_element_type=jnp.float32)
        * factor
    )
    visible = jnp.arange(cache_keys.shape[1])[None, :] < lengths[:, None]
    cached = jnp.where(visible[:, None, None, :], cached, -jnp.inf)
    fresh_scores = (
        jnp.einsum("rkgd,nrkd->rkgn", grouped, new_keys, preferred_element_type=jnp.float32)
        * factor
    )
    highest = jnp.maximum(jnp.max(cached, axis=-1), jnp.max(fresh_scores, axis=-1))
    cached_exp = jnp.exp(cached - highest[..., None])
    fresh_exp = jnp.exp(fresh_scores - highest[..., None])
    totals = jnp.sum(cached_exp, axis=-1) + jnp.sum(fresh_exp, axis=-1)
    cached_prob = (cached_exp / totals[..., None]).astype(jnp.bfloat16)
    fresh_prob = (fresh_exp / totals[..., None]).astype(jnp.bfloat16)
    attended = jnp.einsum(
        "rkgc,rckd->rkgd", cached_prob, stored_cache_values, preferred_element_type=jnp.float32
    )
    attended = attended + jnp.einsum(
        "rkgn,nrkd->rkgd", fresh_prob, new_values, preferred_element_type=jnp.float32
    )
    return attended.reshape(count_of_rows, head_count * head_size).astype(jnp.bfloat16)


def project(normalized_input, query_weight, key_matrix, value_matrix, positions, first_step):
    out_count = lax.axis_size("out")
    inp_count = lax.axis_size("inp")
    inp_index = lax.axis_index("inp")
    step_count = normalized_input.shape[0]
    row_local = normalized_input.shape[1]
    feature_width = normalized_input.shape[2] // inp_count
    own_slice = lax.dynamic_slice_in_dim(
        normalized_input, inp_index * feature_width, feature_width, 2
    )
    query_cols = query_weight.shape[1]
    key_cols = key_matrix.shape[1]
    block_width = query_cols + 2 * key_cols
    shard_rows = lax.all_gather(own_slice, "out", axis=1, tiled=True)
    partials = jnp.concatenate(
        [
            jnp.dot(shard_rows, weight, preferred_element_type=jnp.float32)
            for weight in (query_weight, key_matrix, value_matrix)
        ],
        axis=-1,
    )
    totals = lax.psum(partials, "inp")
    regrouped = lax.all_to_all(totals, "out", split_axis=1, concat_axis=2, tiled=True)
    regrouped = regrouped.reshape(step_count, row_local, out_count, block_width)
    block_count = out_count // inp_count
    summed = lax.dynamic_slice_in_dim(regrouped, inp_index * block_count, block_count, 2)
    query_part = summed[..., :query_cols].reshape(step_count, row_local, -1, HEAD_SIZE)
    key_part = summed[..., query_cols : query_cols + key_cols].reshape(
        step_count, row_local, -1, HEAD_SIZE
    )
    value_part = summed[..., query_cols + key_cols :].reshape(step_count, row_local, -1, HEAD_SIZE)
    placed = positions[None, :] + (first_step + jnp.arange(step_count, dtype=jnp.int32))[:, None]
    queries = rotate(query_part, placed).astype(jnp.bfloat16)
    incoming_keys = rotate(key_part, placed).astype(jnp.bfloat16)
    incoming_values = value_part.astype(jnp.bfloat16)
    return (queries, incoming_keys, incoming_values)


def mix_out(attended, output_weight):
    partials = jnp.dot(
        lax.all_gather(attended, "out", axis=1, tiled=True),
        output_weight,
        preferred_element_type=jnp.float32,
    )
    totals = lax.psum(partials, "inp")
    return lax.all_to_all(
        totals.astype(jnp.bfloat16), "out", split_axis=1, concat_axis=2, tiled=True
    )


ORDERS = ((2, 4, 1), (4, 1, 2))
SETS = ((), (0,), (1,), (2,), (0, 1), (0, 2), (1, 2), (0, 1, 2))
OFFSETS = tuple(tuple(sum(order[n] for n in chosen) for chosen in SETS) for order in ORDERS)


def exchange(block, n):
    pairs = [(2 * o + i, 2 * (o ^ ORDERS[i][n]) + i) for o in range(8) for i in range(2)]
    return lax.ppermute(block, ("out", "inp"), pairs)


def gather_blocks(block, mark):
    a = exchange(block, 0)
    b = exchange(block, 1)
    c = exchange(block, 2)
    c = after(c, mark)
    bc = exchange(b, 2)
    ab = exchange(a, 1)
    ac = exchange(a, 2)
    abc = exchange(ab, 2)
    return block, a, b, c, ab, ac, bc, abc


def swap_cores(block):
    return lax.ppermute(block, "inp", [(0, 1), (1, 0)])


def hand_out(blocks):
    received = []
    for place, block in enumerate(blocks):
        pairs = []
        for o in range(8):
            for i in range(2):
                target = o ^ (4 * i) ^ place
                pairs.append((2 * o + i, 2 * target + o // 4))
        received.append(lax.ppermute(block, ("out", "inp"), pairs))
    return received


def place_of(column):
    return column ^ (lax.axis_index("out") % 4)


VMEM_SPEC = pl.BlockSpec(memory_space=pltpu.VMEM)
SMEM_SPEC = pl.BlockSpec(memory_space=pltpu.SMEM)
MEGABYTE = 1 << 20


def on_chip(kernel, out_shape, scalars, *operands, scratch=(), megabytes=8, moved=1, place=VMEM_SPEC):
    return pl.pallas_call(
        kernel,
        out_shape=out_shape,
        in_specs=[SMEM_SPEC] * len(scalars) + [place] * len(operands),
        out_specs=jax.tree.map(lambda _: VMEM_SPEC, out_shape),
        scratch_shapes=scratch,
        compiler_params=pltpu.CompilerParams(vmem_limit_bytes=megabytes * MEGABYTE),
        cost_estimate=pl.CostEstimate(flops=0, bytes_accessed=moved * MEGABYTE, transcendentals=0),
    )(*scalars, *operands)


def norm_kernel(position_hbm, token_hbm, gain_hbm, out_ref, position_ref, token_ref, gain_ref, arrivals):
    pairs = ((token_hbm, token_ref), (gain_hbm, gain_ref), (position_hbm, position_ref))
    copies = [pltpu.make_async_copy(source, target, arrivals.at[n]) for n, (source, target) in enumerate(pairs)]
    for copy in copies:
        copy.start()
    core = lax.axis_index("inp")
    half = token_ref.shape[1] // 2
    rows = position_ref.shape[0]
    own = pl.ds(pl.multiple_of(core * half, 128), half)
    copies[0].wait()
    values = token_ref[...].astype(jnp.float32)
    factor = lax.rsqrt(jnp.mean(values * values, axis=-1, keepdims=True) + 1e-05)
    copies[1].wait()
    out_ref[:, :half] = (token_ref[:, own].astype(jnp.float32) * factor * gain_ref[:, own]).astype(jnp.bfloat16)
    shape = (token_ref.shape[0], 128)
    row = lax.broadcasted_iota(jnp.int32, shape, 0) % rows
    lane = lax.broadcasted_iota(jnp.int32, shape, 1)
    tag = jnp.zeros(shape, jnp.int32)
    copies[2].wait()
    for r in range(rows):
        place = position_ref[r]
        tag = jnp.where(row == r, jnp.where(lane == 0, place // 128, place % 128), tag)
    out_ref[:, half:] = tag.astype(jnp.float32).astype(jnp.bfloat16)


def fetch_kernel(*refs):
    count = (len(refs) - 2) // 2
    mark_ref, arrivals = refs[-2:]
    copies = []
    for n in range(count):
        source, target = refs[n], refs[count + n]
        size = source.shape[0] // 4
        for part in range(4):
            here = pl.ds(part * size, size)
            copies.append(pltpu.make_async_copy(source.at[here], target.at[here], arrivals.at[n, part]))
    for copy in copies:
        copy.start()
    mark_ref[...] = jnp.zeros_like(mark_ref)
    for copy in copies:
        copy.wait()


def distant(array):
    return pltpu.with_memory_space_constraint(array, pltpu.HBM)


ANYWHERE = pl.BlockSpec(memory_space=pl.ANY)


def fetched(*arrays):
    *near, mark = pl.pallas_call(
        fetch_kernel,
        out_shape=[pltpu.VMEM(array.shape, array.dtype) for array in arrays]
        + [jax.ShapeDtypeStruct((8, 128), jnp.float32)],
        in_specs=[ANYWHERE] * len(arrays),
        out_specs=[VMEM_SPEC] * (len(arrays) + 1),
        scratch_shapes=[pltpu.SemaphoreType.DMA((len(arrays), 4))],
        compiler_params=pltpu.CompilerParams(vmem_limit_bytes=MEGABYTE),
        cost_estimate=pl.CostEstimate(
            flops=0,
            bytes_accessed=sum(array.size * array.dtype.itemsize for array in arrays),
            transcendentals=0,
        ),
    )(*map(distant, arrays))
    return near, mark


def after_kernel(*refs):
    pass


def after(block, *others):
    return pl.pallas_call(
        after_kernel,
        out_shape=jax.ShapeDtypeStruct(block.shape, block.dtype),
        in_specs=[ANYWHERE] * (1 + len(others)),
        out_specs=ANYWHERE,
        input_output_aliases={0: 0},
        compiler_params=pltpu.CompilerParams(vmem_limit_bytes=MEGABYTE),
    )(block, *others)


def stack_rows(pieces, rows_ref):
    core = lax.axis_index("inp")
    rows = pieces[0].shape[0]
    for n, piece in enumerate(pieces):
        offset = jnp.where(core == 0, OFFSETS[0][n] ^ 4, OFFSETS[1][n])
        rows_ref[pl.ds(pl.multiple_of(offset * rows, rows), rows), :] = piece[...]


def project_kernel(*refs):
    pieces, (query_ref, key_ref, value_ref, given_ref, kept_ref, tag_ref, rows_ref) = refs[:8], refs[8:]
    stack_rows(pieces, rows_ref)
    count, depth = given_ref.shape[0], query_ref.shape[0]
    tag_ref[...] = rows_ref[count:, depth:].astype(jnp.float32)
    first = 0
    for weight_ref in (query_ref, key_ref, value_ref):
        width = weight_ref.shape[1]
        block = min(256, width)
        for at in range(0, width, block):
            sums = jnp.dot(rows_ref[:, :depth], weight_ref[:, at : at + block], preferred_element_type=jnp.float32)
            given_ref[:, first + at : first + at + block] = sums[:count]
            kept_ref[:, first + at : first + at + block] = sums[count:]
        first += width


def mix_kernel(*refs):
    pieces, (weight_ref, given_ref, kept_ref, rows_ref) = refs[:8], refs[8:]
    stack_rows(pieces, rows_ref)
    count = given_ref.shape[0]
    for at in range(0, weight_ref.shape[1], 256):
        sums = jnp.dot(rows_ref[...], weight_ref[:, at : at + 256], preferred_element_type=jnp.float32)
        given_ref[:, at : at + 256] = sums[:count]
        kept_ref[:, at : at + 256] = sums[count:]


def turn_kernel(kept_ref, arrived_ref, cosine_ref, sine_ref, *out_refs):
    rows = out_refs[0].shape[0]
    heads = kept_ref.shape[1] // HEAD_SIZE
    for n, out_ref in enumerate(out_refs):
        here = pl.ds(n * rows, rows)
        cosine, sine = cosine_ref[here, :], sine_ref[here, :]
        for head in range(heads):
            columns = slice(head * HEAD_SIZE, (head + 1) * HEAD_SIZE)
            total = kept_ref[here, columns] + arrived_ref[here, columns]
            if head < heads - 1:
                total = total * cosine + pltpu.roll(total, HEAD_SIZE // 2, 1) * sine
            out_ref[:, columns] = total.astype(jnp.bfloat16)


def round_kernel(kept_ref, arrived_ref, *out_refs):
    rows = out_refs[0].shape[0]
    for n, out_ref in enumerate(out_refs):
        total = kept_ref[pl.ds(n * rows, rows), :] + arrived_ref[pl.ds(n * rows, rows), :]
        out_ref[...] = total.astype(jnp.bfloat16)


def place_kernel(own_ref, other_ref, out_ref):
    core = lax.axis_index("inp")
    width = own_ref.shape[2]
    for column in range(4):
        for ref, its_core in ((own_ref, core), (other_ref, 1 - core)):
            start = pl.multiple_of((its_core * 4 + column) * width, width)
            out_ref[:, pl.ds(start, width)] = ref[place_of(column)]


def attend_kernel(length_ref, *refs):
    received, refs = refs[:4], refs[4:]
    keys, values, out_ref, query_rows, fresh_keys, fresh_values, scores = refs
    rows, columns = keys.shape[0], keys.shape[1]
    group = query_rows.shape[2]
    steps = received[0].shape[0] // rows
    asking = steps * group
    for place in range(4):
        block = received[place][...].astype(jnp.float32)
        head = place_of(place)
        for g in range(group):
            query_rows[head, :, g, :] = block[:, g * HEAD_SIZE : (g + 1) * HEAD_SIZE]
        for step in range(steps):
            here = slice(step * rows, (step + 1) * rows)
            fresh_keys[:, step * 4 + head, :] = block[here, group * HEAD_SIZE : (group + 1) * HEAD_SIZE]
            fresh_values[:, step * 4 + head, :] = block[here, (group + 1) * HEAD_SIZE :]
    lane = lax.broadcasted_iota(jnp.int32, (asking, 128), 1)
    own_step = lax.broadcasted_iota(jnp.int32, (asking, 128), 0) // group
    own_lanes = [lane % 4 == head for head in range(4)]
    open_to = (lane < 4 * steps) & (lane // 4 <= own_step)
    across = (((1,), (1,)), ((), ()))
    padding = jnp.zeros((128 - 4 * steps, HEAD_SIZE), jnp.float32)

    def compact(product):
        parts = [product[head * asking : (head + 1) * asking] for head in range(4)]
        return jnp.where(own_lanes[0], parts[0], jnp.where(own_lanes[1], parts[1], jnp.where(own_lanes[2], parts[2], parts[3])))

    def by_head(values, combine):
        for shift in (4, 8, 16, 32, 64):
            values = combine(values, pltpu.roll(values, shift, 1))
        return values

    maxima = []
    for r in range(rows):
        queries = jnp.concatenate(
            [query_rows[head, step * rows + r] for head in range(4) for step in range(steps)]
        ).astype(jnp.bfloat16)
        fresh = jnp.concatenate([fresh_keys[r], padding]).astype(jnp.bfloat16)
        product = lax.dot_general(queries, fresh, across, preferred_element_type=jnp.float32)
        highest = jnp.where(open_to, compact(product), -jnp.inf)
        scores[r, :, columns:] = highest
        for at in range(0, columns, 256):
            product = lax.dot_general(
                queries, keys[r, at : at + 256, :], across, preferred_element_type=jnp.float32
            )
            for start in (at, at + 128):
                part = compact(product[:, start - at : start - at + 128])
                part = jnp.where(lane < 4 * length_ref[r] - start, part, -jnp.inf)
                scores[r, :, start : start + 128] = part
                highest = jnp.maximum(highest, part)
        maxima.append(highest)
    maxima = by_head(jnp.concatenate(maxima), jnp.maximum)
    factor = HEAD_SIZE ** (-0.5) * math.log2(math.e)
    totals = []
    for r in range(rows):
        highest = maxima[r * asking : (r + 1) * asking]
        total = jnp.zeros_like(highest)
        for start in range(0, columns + 128, 128):
            part = jnp.exp2((scores[r, :, start : start + 128] - highest) * factor)
            scores[r, :, start : start + 128] = part
            total += part
        totals.append(total)
    shares = 1.0 / by_head(jnp.concatenate(totals), jnp.add)
    for r in range(rows):
        share = shares[r * asking : (r + 1) * asking]
        spread = []
        for start in range(0, columns + 128, 128):
            part = scores[r, :, start : start + 128] * share
            spread.append(
                jnp.concatenate([jnp.where(own_lanes[head], part, 0.0) for head in range(4)]).astype(jnp.bfloat16)
            )
        fresh = jnp.concatenate([fresh_values[r], padding]).astype(jnp.bfloat16)
        result = jnp.dot(spread[-1], fresh, preferred_element_type=jnp.float32)
        result += jnp.dot(jnp.concatenate(spread[:-1], axis=1), values[r], preferred_element_type=jnp.float32)
        for n in range(4 * steps):
            query_rows[n // steps, n % steps * rows + r] = result[n * group : (n + 1) * group]
    for head in range(4):
        for g in range(group):
            start = (head * group + g) * HEAD_SIZE
            out_ref[:, start : start + HEAD_SIZE] = query_rows[head, :, g, :].astype(jnp.bfloat16)


def attend(received, cache_keys, cache_values, lengths):
    shape = jax.ShapeDtypeStruct
    rows, columns, _ = cache_keys.shape
    key_heads = 4
    count, width = received[0].shape
    group = width // HEAD_SIZE - 2
    fresh = count // rows * key_heads
    return pl.pallas_call(
        attend_kernel,
        out_shape=shape((count, key_heads * group * HEAD_SIZE), jnp.bfloat16),
        in_specs=[SMEM_SPEC] + [VMEM_SPEC] * 6,
        out_specs=VMEM_SPEC,
        scratch_shapes=[
            pltpu.VMEM((key_heads, count, group, HEAD_SIZE), jnp.float32),
            pltpu.VMEM((rows, fresh, HEAD_SIZE), jnp.float32),
            pltpu.VMEM((rows, fresh, HEAD_SIZE), jnp.float32),
            pltpu.VMEM((rows, count // rows * group, columns + 128), jnp.float32),
        ],
        compiler_params=pltpu.CompilerParams(vmem_limit_bytes=6 * MEGABYTE),
        cost_estimate=pl.CostEstimate(flops=0, bytes_accessed=12 * MEGABYTE, transcendentals=0),
    )(lengths, *received, resident(cache_keys), resident(cache_values))


def resident(array):
    return pltpu.with_memory_space_constraint(array, pltpu.VMEM)


def eight_chip_body(
    tokens, norm_gain, query_weight, key_matrix, value_matrix, output_weight, cache_keys, cache_values, lengths, positions
):
    steps, rows, width = tokens.shape
    count = steps * rows
    half = width // 2
    core = lax.axis_index("inp")
    query_cols = query_weight.shape[1]
    qkv_cols = query_cols + 2 * key_matrix.shape[1]
    shape = jax.ShapeDtypeStruct
    own = on_chip(
        norm_kernel,
        shape((count, half + 128), jnp.bfloat16),
        (),
        distant(positions),
        distant(tokens.reshape(count, width)),
        distant(norm_gain.reshape(1, width)),
        scratch=[
            pltpu.SMEM((rows,), jnp.int32),
            pltpu.VMEM((count, width), jnp.bfloat16),
            pltpu.VMEM((1, width), jnp.float32),
            pltpu.SemaphoreType.DMA((3,)),
        ],
        place=pl.BlockSpec(memory_space=pltpu.HBM),
    )
    (near_query, near_key, near_value), weight_mark = fetched(query_weight, key_matrix, value_matrix)
    (near_keys, near_values), cache_mark = fetched(
        cache_keys.reshape(rows, -1, HEAD_SIZE), cache_values.reshape(rows, -1, HEAD_SIZE)
    )
    blocks = gather_blocks(own, weight_mark)
    given, kept, tags = on_chip(
        project_kernel,
        [shape((4 * count, qkv_cols), jnp.float32)] * 2 + [shape((4 * count, 128), jnp.float32)],
        (),
        *blocks,
        resident(near_query),
        resident(near_key),
        resident(near_value),
        scratch=[pltpu.VMEM((8 * count, half + 128), jnp.bfloat16)],
    )
    arrived = swap_cores(given)
    frequency = jnp.exp(
        -math.log(500000.0) * 2.0 * jnp.arange(HEAD_SIZE // 2, dtype=jnp.float32) / HEAD_SIZE
    )
    step = (jnp.arange(4 * count) // rows % steps).astype(jnp.float32)
    angles = (tags[:, 0] * 128.0 + tags[:, 1] + step)[:, None] * frequency
    cosine, sine = jnp.cos(angles), jnp.sin(angles)
    outgoing = on_chip(
        turn_kernel,
        [shape((count, qkv_cols), jnp.bfloat16)] * 4,
        (),
        kept,
        arrived,
        jnp.concatenate([cosine, cosine], axis=-1),
        jnp.concatenate([-sine, sine], axis=-1),
    )
    attended = attend(hand_out(outgoing), near_keys, near_values, lengths)
    (near_output,), output_mark = fetched(output_weight)
    blocks = gather_blocks(attended, output_mark)
    mix_cols = output_weight.shape[1]
    given, kept = on_chip(
        mix_kernel,
        [shape((4 * count, mix_cols), jnp.float32)] * 2,
        (),
        *blocks,
        resident(near_output),
        scratch=[pltpu.VMEM((8 * count, half), jnp.bfloat16)],
    )
    outgoing = on_chip(
        round_kernel, [shape((count, mix_cols), jnp.bfloat16)] * 4, (), kept, swap_cores(given)
    )
    own_half = jnp.stack(hand_out(outgoing))
    mixed = on_chip(
        place_kernel,
        shape((count, width), jnp.bfloat16),
        (),
        own_half,
        swap_cores(own_half),
    )
    return mixed.reshape(steps, rows, width)


def body(
    tokens,
    norm_gain,
    query_weight,
    key_matrix,
    value_matrix,
    output_weight,
    cache_keys,
    stored_cache_values,
    lengths,
    positions,
):
    normalized_input = rms_normed(tokens, norm_gain)
    key_list = []
    value_list = []
    results = []
    for token_step in range(2):
        queries, incoming_keys, incoming_values = project(
            normalized_input[token_step : token_step + 1],
            query_weight,
            key_matrix,
            value_matrix,
            positions,
            token_step,
        )
        key_list.append(incoming_keys[0])
        value_list.append(incoming_values[0])
        attended = attend_one(
            queries[0],
            jnp.stack(key_list),
            jnp.stack(value_list),
            cache_keys,
            stored_cache_values,
            lengths,
        )
        results.append(mix_out(attended[None], output_weight)[0])
    return jnp.stack(results)


def solution(mesh):
    placed = (
        P(None, ("group", "out"), None),
        P(),
        P("inp", "out"),
        P("inp", "out"),
        P("inp", "out"),
        P("inp", "out"),
        P(("group", "out"), None, "inp", None),
        P(("group", "out"), None, "inp", None),
        P(("group", "out")),
        P(("group", "out")),
    )
    chosen = eight_chip_body if (mesh.shape["out"], mesh.shape["inp"]) == (8, 2) else body
    return jax.shard_map(
        chosen, mesh=mesh, in_specs=placed, out_specs=P(None, ("group", "out"), None), check_vma=False
    )
```

```python
import functools
import math

import jax
import jax.numpy as jnp
from jax import lax
from jax.experimental import pallas as pl
from jax.experimental.pallas import tpu as pltpu
from jax.sharding import PartitionSpec as P

HEAD_SIZE = 128


def rms_normed(tokens, gain):
    values = tokens.astype(jnp.float32)
    factor = lax.rsqrt(jnp.mean(values * values, axis=-1, keepdims=True) + 1e-05)
    return (values * factor * gain).astype(jnp.bfloat16)


def rotate(heads, position):
    head_size = heads.shape[-1]
    half_size = head_size // 2
    frequency = jnp.exp(
        -math.log(500000.0) * 2.0 * jnp.arange(half_size, dtype=jnp.float32) / head_size
    )
    angles = position.astype(jnp.float32)[..., None, None] * frequency
    cosine = jnp.cos(angles)
    sine_part = jnp.sin(angles)
    leading = heads[..., :half_size]
    trailing = heads[..., half_size:]
    return jnp.concatenate(
        [leading * cosine - trailing * sine_part, trailing * cosine + leading * sine_part], axis=-1
    )


def attend_one(queries, new_keys, new_values, cache_keys, stored_cache_values, lengths):
    count_of_rows, head_count, head_size = queries.shape
    key_heads = cache_keys.shape[2]
    grouped = queries.reshape(count_of_rows, key_heads, head_count // key_heads, head_size)
    factor = head_size ** (-0.5)
    cached = (
        jnp.einsum("rkgd,rckd->rkgc", grouped, cache_keys, preferred_element_type=jnp.float32)
        * factor
    )
    visible = jnp.arange(cache_keys.shape[1])[None, :] < lengths[:, None]
    cached = jnp.where(visible[:, None, None, :], cached, -jnp.inf)
    fresh_scores = (
        jnp.einsum("rkgd,nrkd->rkgn", grouped, new_keys, preferred_element_type=jnp.float32)
        * factor
    )
    highest = jnp.maximum(jnp.max(cached, axis=-1), jnp.max(fresh_scores, axis=-1))
    cached_exp = jnp.exp(cached - highest[..., None])
    fresh_exp = jnp.exp(fresh_scores - highest[..., None])
    totals = jnp.sum(cached_exp, axis=-1) + jnp.sum(fresh_exp, axis=-1)
    cached_prob = (cached_exp / totals[..., None]).astype(jnp.bfloat16)
    fresh_prob = (fresh_exp / totals[..., None]).astype(jnp.bfloat16)
    attended = jnp.einsum(
        "rkgc,rckd->rkgd", cached_prob, stored_cache_values, preferred_element_type=jnp.float32
    )
    attended = attended + jnp.einsum(
        "rkgn,nrkd->rkgd", fresh_prob, new_values, preferred_element_type=jnp.float32
    )
    return attended.reshape(count_of_rows, head_count * head_size).astype(jnp.bfloat16)


def project(normalized_input, query_weight, key_matrix, value_matrix, positions, first_step):
    out_count = lax.axis_size("out")
    inp_count = lax.axis_size("inp")
    inp_index = lax.axis_index("inp")
    step_count = normalized_input.shape[0]
    row_local = normalized_input.shape[1]
    feature_width = normalized_input.shape[2] // inp_count
    own_slice = lax.dynamic_slice_in_dim(
        normalized_input, inp_index * feature_width, feature_width, 2
    )
    query_cols = query_weight.shape[1]
    key_cols = key_matrix.shape[1]
    block_width = query_cols + 2 * key_cols
    shard_rows = lax.all_gather(own_slice, "out", axis=1, tiled=True)
    partials = jnp.concatenate(
        [
            jnp.dot(shard_rows, weight, preferred_element_type=jnp.float32)
            for weight in (query_weight, key_matrix, value_matrix)
        ],
        axis=-1,
    )
    totals = lax.psum(partials, "inp")
    regrouped = lax.all_to_all(totals, "out", split_axis=1, concat_axis=2, tiled=True)
    regrouped = regrouped.reshape(step_count, row_local, out_count, block_width)
    block_count = out_count // inp_count
    summed = lax.dynamic_slice_in_dim(regrouped, inp_index * block_count, block_count, 2)
    query_part = summed[..., :query_cols].reshape(step_count, row_local, -1, HEAD_SIZE)
    key_part = summed[..., query_cols : query_cols + key_cols].reshape(
        step_count, row_local, -1, HEAD_SIZE
    )
    value_part = summed[..., query_cols + key_cols :].reshape(step_count, row_local, -1, HEAD_SIZE)
    placed = positions[None, :] + (first_step + jnp.arange(step_count, dtype=jnp.int32))[:, None]
    queries = rotate(query_part, placed).astype(jnp.bfloat16)
    incoming_keys = rotate(key_part, placed).astype(jnp.bfloat16)
    incoming_values = value_part.astype(jnp.bfloat16)
    return (queries, incoming_keys, incoming_values)


def mix_out(attended, output_weight):
    partials = jnp.dot(
        lax.all_gather(attended, "out", axis=1, tiled=True),
        output_weight,
        preferred_element_type=jnp.float32,
    )
    totals = lax.psum(partials, "inp")
    return lax.all_to_all(
        totals.astype(jnp.bfloat16), "out", split_axis=1, concat_axis=2, tiled=True
    )


ORDERS = ((2, 4, 1), (4, 1, 2))
SETS = ((), (0,), (1,), (2,), (0, 1), (0, 2), (1, 2), (0, 1, 2))
OFFSETS = tuple(tuple(sum(order[n] for n in chosen) for chosen in SETS) for order in ORDERS)


def exchange(block, n):
    pairs = [(2 * o + i, 2 * (o ^ ORDERS[i][n]) + i) for o in range(8) for i in range(2)]
    return lax.ppermute(block, ("out", "inp"), pairs)


def gather_blocks(block, early, late):
    a = exchange(block, 0)
    b = exchange(block, 1)
    c = exchange(block, 2)
    a = a if early is None else after(a, early)
    bc = exchange(b, 2)
    ab = exchange(a, 1)
    ac = exchange(a, 2)
    abc = exchange(ab, 2)
    ac = ac if late is None else after(ac, late)
    return block, a, b, c, ab, ac, bc, abc


def swap_cores(block):
    return lax.ppermute(block, "inp", [(0, 1), (1, 0)])


def hand_out(blocks):
    received = []
    for place, block in enumerate(blocks):
        pairs = []
        for o in range(8):
            for i in range(2):
                target = o ^ (4 * i) ^ place
                pairs.append((2 * o + i, 2 * target + o // 4))
        received.append(lax.ppermute(block, ("out", "inp"), pairs))
    return received


def place_of(column):
    return column ^ (lax.axis_index("out") % 4)


VMEM_SPEC = pl.BlockSpec(memory_space=pltpu.VMEM)
SMEM_SPEC = pl.BlockSpec(memory_space=pltpu.SMEM)
MEGABYTE = 1 << 20


def on_chip(kernel, out_shape, scalars, *operands, scratch=(), megabytes=8, moved=1, place=VMEM_SPEC):
    return pl.pallas_call(
        kernel,
        out_shape=out_shape,
        in_specs=[SMEM_SPEC] * len(scalars) + [place] * len(operands),
        out_specs=jax.tree.map(lambda _: VMEM_SPEC, out_shape),
        scratch_shapes=scratch,
        compiler_params=pltpu.CompilerParams(vmem_limit_bytes=megabytes * MEGABYTE),
        cost_estimate=pl.CostEstimate(flops=0, bytes_accessed=moved * MEGABYTE, transcendentals=0),
    )(*scalars, *operands)


def norm_kernel(position_hbm, token_hbm, gain_hbm, out_ref, position_ref, token_ref, gain_ref, arrivals):
    pairs = ((token_hbm, token_ref), (gain_hbm, gain_ref), (position_hbm, position_ref))
    copies = [pltpu.make_async_copy(source, target, arrivals.at[n]) for n, (source, target) in enumerate(pairs)]
    for copy in copies:
        copy.start()
    core = lax.axis_index("inp")
    half = token_ref.shape[1] // 2
    rows = position_ref.shape[0]
    own = pl.ds(pl.multiple_of(core * half, 128), half)
    copies[0].wait()
    values = token_ref[...].astype(jnp.float32)
    factor = lax.rsqrt(jnp.mean(values * values, axis=-1, keepdims=True) + 1e-05)
    copies[1].wait()
    out_ref[:, :half] = (token_ref[:, own].astype(jnp.float32) * factor * gain_ref[:, own]).astype(jnp.bfloat16)
    shape = (token_ref.shape[0], 128)
    row = lax.broadcasted_iota(jnp.int32, shape, 0) % rows
    lane = lax.broadcasted_iota(jnp.int32, shape, 1)
    tag = jnp.zeros(shape, jnp.int32)
    copies[2].wait()
    for r in range(rows):
        place = position_ref[r]
        tag = jnp.where(row == r, jnp.where(lane == 0, place // 128, place % 128), tag)
    out_ref[:, half:] = tag.astype(jnp.float32).astype(jnp.bfloat16)


def fetch_kernel(starts, *refs):
    count = (len(refs) - 2) // 2
    mark_ref, arrivals = refs[-2:]
    copies = []
    for n in range(count):
        source, target = refs[n], refs[count + n]
        size = target.shape[0] // 4
        for part in range(4):
            there, here = pl.ds(starts[n] + part * size, size), pl.ds(part * size, size)
            copies.append(pltpu.make_async_copy(source.at[there], target.at[here], arrivals.at[n, part]))
    for copy in copies:
        copy.start()
    mark_ref[...] = jnp.zeros_like(mark_ref)
    for copy in copies:
        copy.wait()


def distant(array):
    return pltpu.with_memory_space_constraint(array, pltpu.HBM)


ANYWHERE = pl.BlockSpec(memory_space=pl.ANY)


def fetched(*parts):
    shapes = [(rows,) + array.shape[1:] for array, _, rows in parts]
    *near, mark = pl.pallas_call(
        functools.partial(fetch_kernel, [start for _, start, _ in parts]),
        out_shape=[pltpu.VMEM(shape, part[0].dtype) for shape, part in zip(shapes, parts)]
        + [jax.ShapeDtypeStruct((8, 128), jnp.float32)],
        in_specs=[ANYWHERE] * len(parts),
        out_specs=[VMEM_SPEC] * (len(parts) + 1),
        scratch_shapes=[pltpu.SemaphoreType.DMA((len(parts), 4))],
        compiler_params=pltpu.CompilerParams(vmem_limit_bytes=MEGABYTE),
        cost_estimate=pl.CostEstimate(
            flops=0, bytes_accessed=sum(2 * math.prod(shape) for shape in shapes), transcendentals=0
        ),
    )(*[distant(array) for array, _, _ in parts])
    return near, mark


def after_kernel(*refs):
    pass


def after(block, *others):
    return pl.pallas_call(
        after_kernel,
        out_shape=jax.ShapeDtypeStruct(block.shape, block.dtype),
        in_specs=[ANYWHERE] * (1 + len(others)),
        out_specs=ANYWHERE,
        input_output_aliases={0: 0},
        compiler_params=pltpu.CompilerParams(vmem_limit_bytes=MEGABYTE),
    )(block, *others)


def stack_rows(pieces, rows_ref):
    core = lax.axis_index("inp")
    rows = pieces[0].shape[0]
    for n, piece in enumerate(pieces):
        offset = jnp.where(core == 0, OFFSETS[0][n] ^ 4, OFFSETS[1][n])
        rows_ref[pl.ds(pl.multiple_of(offset * rows, rows), rows), :] = piece[...]


def multiply(rows_ref, weights, at, block):
    total, first = 0.0, 0
    for weight in weights:
        depth = weight.shape[0]
        total += jnp.dot(
            rows_ref[:, first : first + depth], weight[:, at : at + block], preferred_element_type=jnp.float32
        )
        first += depth
    return total


def project_kernel(*refs):
    pieces, key_ref, value_ref, queries = refs[:8], refs[8], refs[9], refs[10:-4]
    given_ref, kept_ref, tag_ref, rows_ref = refs[-4:]
    stack_rows(pieces, rows_ref)
    count, depth = given_ref.shape[0], key_ref.shape[0]
    tag_ref[...] = rows_ref[count:, depth:].astype(jnp.float32)
    first = 0
    for weights in (queries, (key_ref,), (value_ref,)):
        width = weights[0].shape[1]
        block = min(256, width)
        for at in range(0, width, block):
            sums = multiply(rows_ref, weights, at, block)
            given_ref[:, first + at : first + at + block] = sums[:count]
            kept_ref[:, first + at : first + at + block] = sums[count:]
        first += width


def mix_kernel(*refs):
    pieces, weights, (given_ref, kept_ref, rows_ref) = refs[:8], refs[8:-3], refs[-3:]
    stack_rows(pieces, rows_ref)
    count = given_ref.shape[0]
    for at in range(0, weights[0].shape[1], 256):
        sums = multiply(rows_ref, weights, at, 256)
        given_ref[:, at : at + 256] = sums[:count]
        kept_ref[:, at : at + 256] = sums[count:]


def turn_kernel(kept_ref, arrived_ref, cosine_ref, sine_ref, *out_refs):
    rows = out_refs[0].shape[0]
    heads = kept_ref.shape[1] // HEAD_SIZE
    for n, out_ref in enumerate(out_refs):
        here = pl.ds(n * rows, rows)
        cosine, sine = cosine_ref[here, :], sine_ref[here, :]
        for head in range(heads):
            columns = slice(head * HEAD_SIZE, (head + 1) * HEAD_SIZE)
            total = kept_ref[here, columns] + arrived_ref[here, columns]
            if head < heads - 1:
                total = total * cosine + pltpu.roll(total, HEAD_SIZE // 2, 1) * sine
            out_ref[:, columns] = total.astype(jnp.bfloat16)


def round_kernel(kept_ref, arrived_ref, *out_refs):
    rows = out_refs[0].shape[0]
    for n, out_ref in enumerate(out_refs):
        total = kept_ref[pl.ds(n * rows, rows), :] + arrived_ref[pl.ds(n * rows, rows), :]
        out_ref[...] = total.astype(jnp.bfloat16)


def place_kernel(own_ref, other_ref, out_ref):
    core = lax.axis_index("inp")
    width = own_ref.shape[2]
    for column in range(4):
        for ref, its_core in ((own_ref, core), (other_ref, 1 - core)):
            start = pl.multiple_of((its_core * 4 + column) * width, width)
            out_ref[:, pl.ds(start, width)] = ref[place_of(column)]


def attend_kernel(length_ref, *refs):
    received, refs = refs[:4], refs[4:]
    keys, values, out_ref, query_rows, fresh_keys, fresh_values, scores = refs
    rows, columns = keys.shape[0], keys.shape[1]
    group = query_rows.shape[2]
    steps = received[0].shape[0] // rows
    asking = steps * group
    for place in range(4):
        block = received[place][...].astype(jnp.float32)
        head = place_of(place)
        for g in range(group):
            query_rows[head, :, g, :] = block[:, g * HEAD_SIZE : (g + 1) * HEAD_SIZE]
        for step in range(steps):
            here = slice(step * rows, (step + 1) * rows)
            fresh_keys[:, step * 4 + head, :] = block[here, group * HEAD_SIZE : (group + 1) * HEAD_SIZE]
            fresh_values[:, step * 4 + head, :] = block[here, (group + 1) * HEAD_SIZE :]
    lane = lax.broadcasted_iota(jnp.int32, (asking, 128), 1)
    own_step = lax.broadcasted_iota(jnp.int32, (asking, 128), 0) // group
    own_lanes = [lane % 4 == head for head in range(4)]
    open_to = (lane < 4 * steps) & (lane // 4 <= own_step)
    across = (((1,), (1,)), ((), ()))
    padding = jnp.zeros((128 - 4 * steps, HEAD_SIZE), jnp.float32)

    def compact(product):
        parts = [product[head * asking : (head + 1) * asking] for head in range(4)]
        return jnp.where(own_lanes[0], parts[0], jnp.where(own_lanes[1], parts[1], jnp.where(own_lanes[2], parts[2], parts[3])))

    def by_head(values, combine):
        for shift in (4, 8, 16, 32, 64):
            values = combine(values, pltpu.roll(values, shift, 1))
        return values

    maxima = []
    for r in range(rows):
        queries = jnp.concatenate(
            [query_rows[head, step * rows + r] for head in range(4) for step in range(steps)]
        ).astype(jnp.bfloat16)
        fresh = jnp.concatenate([fresh_keys[r], padding]).astype(jnp.bfloat16)
        product = lax.dot_general(queries, fresh, across, preferred_element_type=jnp.float32)
        highest = jnp.where(open_to, compact(product), -jnp.inf)
        scores[r, :, columns:] = highest
        for at in range(0, columns, 256):
            product = lax.dot_general(
                queries, keys[r, at : at + 256, :], across, preferred_element_type=jnp.float32
            )
            for start in (at, at + 128):
                part = compact(product[:, start - at : start - at + 128])
                part = jnp.where(lane < 4 * length_ref[r] - start, part, -jnp.inf)
                scores[r, :, start : start + 128] = part
                highest = jnp.maximum(highest, part)
        maxima.append(highest)
    maxima = by_head(jnp.concatenate(maxima), jnp.maximum)
    factor = HEAD_SIZE ** (-0.5) * math.log2(math.e)
    totals = []
    for r in range(rows):
        highest = maxima[r * asking : (r + 1) * asking]
        total = jnp.zeros_like(highest)
        for start in range(0, columns + 128, 128):
            part = jnp.exp2((scores[r, :, start : start + 128] - highest) * factor)
            scores[r, :, start : start + 128] = part
            total += part
        totals.append(total)
    shares = 1.0 / by_head(jnp.concatenate(totals), jnp.add)
    for r in range(rows):
        share = shares[r * asking : (r + 1) * asking]
        spread = []
        for start in range(0, columns + 128, 128):
            part = scores[r, :, start : start + 128] * share
            spread.append(
                jnp.concatenate([jnp.where(own_lanes[head], part, 0.0) for head in range(4)]).astype(jnp.bfloat16)
            )
        fresh = jnp.concatenate([fresh_values[r], padding]).astype(jnp.bfloat16)
        result = jnp.dot(spread[-1], fresh, preferred_element_type=jnp.float32)
        result += jnp.dot(jnp.concatenate(spread[:-1], axis=1), values[r], preferred_element_type=jnp.float32)
        for n in range(4 * steps):
            query_rows[n // steps, n % steps * rows + r] = result[n * group : (n + 1) * group]
    for head in range(4):
        for g in range(group):
            start = (head * group + g) * HEAD_SIZE
            out_ref[:, start : start + HEAD_SIZE] = query_rows[head, :, g, :].astype(jnp.bfloat16)


def attend(received, cache_keys, cache_values, lengths):
    shape = jax.ShapeDtypeStruct
    rows, columns, _ = cache_keys.shape
    key_heads = 4
    count, width = received[0].shape
    group = width // HEAD_SIZE - 2
    fresh = count // rows * key_heads
    return pl.pallas_call(
        attend_kernel,
        out_shape=shape((count, key_heads * group * HEAD_SIZE), jnp.bfloat16),
        in_specs=[SMEM_SPEC] + [VMEM_SPEC] * 6,
        out_specs=VMEM_SPEC,
        scratch_shapes=[
            pltpu.VMEM((key_heads, count, group, HEAD_SIZE), jnp.float32),
            pltpu.VMEM((rows, fresh, HEAD_SIZE), jnp.float32),
            pltpu.VMEM((rows, fresh, HEAD_SIZE), jnp.float32),
            pltpu.VMEM((rows, count // rows * group, columns + 128), jnp.float32),
        ],
        compiler_params=pltpu.CompilerParams(vmem_limit_bytes=6 * MEGABYTE),
        cost_estimate=pl.CostEstimate(flops=0, bytes_accessed=12 * MEGABYTE, transcendentals=0),
    )(lengths, *received, resident(cache_keys), resident(cache_values))


def resident(array):
    return pltpu.with_memory_space_constraint(array, pltpu.VMEM)


def eight_chip_body(
    tokens, norm_gain, query_weight, key_matrix, value_matrix, output_weight, cache_keys, cache_values, lengths, positions
):
    steps, rows, width = tokens.shape
    count = steps * rows
    half = width // 2
    core = lax.axis_index("inp")
    query_cols = query_weight.shape[1]
    qkv_cols = query_cols + 2 * key_matrix.shape[1]
    shape = jax.ShapeDtypeStruct
    own = on_chip(
        norm_kernel,
        shape((count, half + 128), jnp.bfloat16),
        (),
        distant(positions),
        distant(tokens.reshape(count, width)),
        distant(norm_gain.reshape(1, width)),
        scratch=[
            pltpu.SMEM((rows,), jnp.int32),
            pltpu.VMEM((count, width), jnp.bfloat16),
            pltpu.VMEM((1, width), jnp.float32),
            pltpu.SemaphoreType.DMA((3,)),
        ],
        place=pl.BlockSpec(memory_space=pltpu.HBM),
    )
    depth = query_weight.shape[0]
    (query_first, near_key, near_value,), early = fetched((query_weight, 0, depth * 2048 // 4096), (key_matrix, 0, depth), (value_matrix, 0, depth))
    (query_second,), late = fetched((query_weight, depth * 2048 // 4096, depth - depth * 2048 // 4096))
    (near_keys, near_values), cache_mark = fetched(
        (cache_keys.reshape(rows, -1, HEAD_SIZE), 0, rows), (cache_values.reshape(rows, -1, HEAD_SIZE), 0, rows)
    )
    blocks = gather_blocks(own, early, late)
    given, kept, tags = on_chip(
        project_kernel,
        [shape((4 * count, qkv_cols), jnp.float32)] * 2 + [shape((4 * count, 128), jnp.float32)],
        (),
        *blocks,
        resident(near_key),
        resident(near_value),
        resident(query_first),
        resident(query_second),
        scratch=[pltpu.VMEM((8 * count, half + 128), jnp.bfloat16)],
    )
    arrived = swap_cores(given)
    frequency = jnp.exp(
        -math.log(500000.0) * 2.0 * jnp.arange(HEAD_SIZE // 2, dtype=jnp.float32) / HEAD_SIZE
    )
    step = (jnp.arange(4 * count) // rows % steps).astype(jnp.float32)
    angles = (tags[:, 0] * 128.0 + tags[:, 1] + step)[:, None] * frequency
    cosine, sine = jnp.cos(angles), jnp.sin(angles)
    outgoing = on_chip(
        turn_kernel,
        [shape((count, qkv_cols), jnp.bfloat16)] * 4,
        (),
        kept,
        arrived,
        jnp.concatenate([cosine, cosine], axis=-1),
        jnp.concatenate([-sine, sine], axis=-1),
    )
    attended = attend(hand_out(outgoing), near_keys, near_values, lengths)
    (output_first,), early = fetched((output_weight, 0, depth * 2048 // 4096))
    (output_second,), late = fetched((output_weight, depth * 2048 // 4096, depth - depth * 2048 // 4096))
    blocks = gather_blocks(attended, early, late)
    mix_cols = output_weight.shape[1]
    given, kept = on_chip(
        mix_kernel,
        [shape((4 * count, mix_cols), jnp.float32)] * 2,
        (),
        *blocks,
        resident(output_first),
        resident(output_second),
        scratch=[pltpu.VMEM((8 * count, half), jnp.bfloat16)],
    )
    outgoing = on_chip(
        round_kernel, [shape((count, mix_cols), jnp.bfloat16)] * 4, (), kept, swap_cores(given)
    )
    own_half = jnp.stack(hand_out(outgoing))
    mixed = on_chip(
        place_kernel,
        shape((count, width), jnp.bfloat16),
        (),
        own_half,
        swap_cores(own_half),
    )
    return mixed.reshape(steps, rows, width)


def body(
    tokens,
    norm_gain,
    query_weight,
    key_matrix,
    value_matrix,
    output_weight,
    cache_keys,
    stored_cache_values,
    lengths,
    positions,
):
    normalized_input = rms_normed(tokens, norm_gain)
    key_list = []
    value_list = []
    results = []
    for token_step in range(2):
        queries, incoming_keys, incoming_values = project(
            normalized_input[token_step : token_step + 1],
            query_weight,
            key_matrix,
            value_matrix,
            positions,
            token_step,
        )
        key_list.append(incoming_keys[0])
        value_list.append(incoming_values[0])
        attended = attend_one(
            queries[0],
            jnp.stack(key_list),
            jnp.stack(value_list),
            cache_keys,
            stored_cache_values,
            lengths,
        )
        results.append(mix_out(attended[None], output_weight)[0])
    return jnp.stack(results)


def solution(mesh):
    placed = (
        P(None, ("group", "out"), None),
        P(),
        P("inp", "out"),
        P("inp", "out"),
        P("inp", "out"),
        P("inp", "out"),
        P(("group", "out"), None, "inp", None),
        P(("group", "out"), None, "inp", None),
        P(("group", "out")),
        P(("group", "out")),
    )
    chosen = eight_chip_body if (mesh.shape["out"], mesh.shape["inp"]) == (8, 2) else body
    return jax.shard_map(
        chosen, mesh=mesh, in_specs=placed, out_specs=P(None, ("group", "out"), None), check_vma=False
    )
```

```python
import functools
import math

import jax
import jax.numpy as jnp
from jax import lax
from jax.experimental import pallas as pl
from jax.experimental.pallas import tpu as pltpu
from jax.sharding import PartitionSpec as P

HEAD_SIZE = 128


def rms_normed(tokens, gain):
    values = tokens.astype(jnp.float32)
    factor = lax.rsqrt(jnp.mean(values * values, axis=-1, keepdims=True) + 1e-05)
    return (values * factor * gain).astype(jnp.bfloat16)


def rotate(heads, position):
    head_size = heads.shape[-1]
    half_size = head_size // 2
    frequency = jnp.exp(
        -math.log(500000.0) * 2.0 * jnp.arange(half_size, dtype=jnp.float32) / head_size
    )
    angles = position.astype(jnp.float32)[..., None, None] * frequency
    cosine = jnp.cos(angles)
    sine_part = jnp.sin(angles)
    leading = heads[..., :half_size]
    trailing = heads[..., half_size:]
    return jnp.concatenate(
        [leading * cosine - trailing * sine_part, trailing * cosine + leading * sine_part], axis=-1
    )


def attend_one(queries, new_keys, new_values, cache_keys, stored_cache_values, lengths):
    count_of_rows, head_count, head_size = queries.shape
    key_heads = cache_keys.shape[2]
    grouped = queries.reshape(count_of_rows, key_heads, head_count // key_heads, head_size)
    factor = head_size ** (-0.5)
    cached = (
        jnp.einsum("rkgd,rckd->rkgc", grouped, cache_keys, preferred_element_type=jnp.float32)
        * factor
    )
    visible = jnp.arange(cache_keys.shape[1])[None, :] < lengths[:, None]
    cached = jnp.where(visible[:, None, None, :], cached, -jnp.inf)
    fresh_scores = (
        jnp.einsum("rkgd,nrkd->rkgn", grouped, new_keys, preferred_element_type=jnp.float32)
        * factor
    )
    highest = jnp.maximum(jnp.max(cached, axis=-1), jnp.max(fresh_scores, axis=-1))
    cached_exp = jnp.exp(cached - highest[..., None])
    fresh_exp = jnp.exp(fresh_scores - highest[..., None])
    totals = jnp.sum(cached_exp, axis=-1) + jnp.sum(fresh_exp, axis=-1)
    cached_prob = (cached_exp / totals[..., None]).astype(jnp.bfloat16)
    fresh_prob = (fresh_exp / totals[..., None]).astype(jnp.bfloat16)
    attended = jnp.einsum(
        "rkgc,rckd->rkgd", cached_prob, stored_cache_values, preferred_element_type=jnp.float32
    )
    attended = attended + jnp.einsum(
        "rkgn,nrkd->rkgd", fresh_prob, new_values, preferred_element_type=jnp.float32
    )
    return attended.reshape(count_of_rows, head_count * head_size).astype(jnp.bfloat16)


def project(normalized_input, query_weight, key_matrix, value_matrix, positions, first_step):
    out_count = lax.axis_size("out")
    inp_count = lax.axis_size("inp")
    inp_index = lax.axis_index("inp")
    step_count = normalized_input.shape[0]
    row_local = normalized_input.shape[1]
    feature_width = normalized_input.shape[2] // inp_count
    own_slice = lax.dynamic_slice_in_dim(
        normalized_input, inp_index * feature_width, feature_width, 2
    )
    query_cols = query_weight.shape[1]
    key_cols = key_matrix.shape[1]
    block_width = query_cols + 2 * key_cols
    shard_rows = lax.all_gather(own_slice, "out", axis=1, tiled=True)
    partials = jnp.concatenate(
        [
            jnp.dot(shard_rows, weight, preferred_element_type=jnp.float32)
            for weight in (query_weight, key_matrix, value_matrix)
        ],
        axis=-1,
    )
    totals = lax.psum(partials, "inp")
    regrouped = lax.all_to_all(totals, "out", split_axis=1, concat_axis=2, tiled=True)
    regrouped = regrouped.reshape(step_count, row_local, out_count, block_width)
    block_count = out_count // inp_count
    summed = lax.dynamic_slice_in_dim(regrouped, inp_index * block_count, block_count, 2)
    query_part = summed[..., :query_cols].reshape(step_count, row_local, -1, HEAD_SIZE)
    key_part = summed[..., query_cols : query_cols + key_cols].reshape(
        step_count, row_local, -1, HEAD_SIZE
    )
    value_part = summed[..., query_cols + key_cols :].reshape(step_count, row_local, -1, HEAD_SIZE)
    placed = positions[None, :] + (first_step + jnp.arange(step_count, dtype=jnp.int32))[:, None]
    queries = rotate(query_part, placed).astype(jnp.bfloat16)
    incoming_keys = rotate(key_part, placed).astype(jnp.bfloat16)
    incoming_values = value_part.astype(jnp.bfloat16)
    return (queries, incoming_keys, incoming_values)


def mix_out(attended, output_weight):
    partials = jnp.dot(
        lax.all_gather(attended, "out", axis=1, tiled=True),
        output_weight,
        preferred_element_type=jnp.float32,
    )
    totals = lax.psum(partials, "inp")
    return lax.all_to_all(
        totals.astype(jnp.bfloat16), "out", split_axis=1, concat_axis=2, tiled=True
    )


ORDERS = ((2, 4, 1), (4, 1, 2))
SETS = ((), (0,), (1,), (2,), (0, 1), (0, 2), (1, 2), (0, 1, 2))
OFFSETS = tuple(tuple(sum(order[n] for n in chosen) for chosen in SETS) for order in ORDERS)


def exchange(block, n):
    pairs = [(2 * o + i, 2 * (o ^ ORDERS[i][n]) + i) for o in range(8) for i in range(2)]
    return lax.ppermute(block, ("out", "inp"), pairs)


def gather_blocks(block, early, late):
    a = exchange(block, 0)
    b = exchange(block, 1)
    c = exchange(block, 2)
    a = a if early is None else after(a, early)
    bc = exchange(b, 2)
    ab = exchange(a, 1)
    ac = exchange(a, 2)
    abc = exchange(ab, 2)
    ac = ac if late is None else after(ac, late)
    return block, a, b, c, ab, ac, bc, abc


def swap_cores(block):
    return lax.ppermute(block, "inp", [(0, 1), (1, 0)])


def hand_out(blocks):
    received = []
    for place, block in enumerate(blocks):
        pairs = []
        for o in range(8):
            for i in range(2):
                target = o ^ (4 * i) ^ place
                pairs.append((2 * o + i, 2 * target + o // 4))
        received.append(lax.ppermute(block, ("out", "inp"), pairs))
    return received


def place_of(column):
    return column ^ (lax.axis_index("out") % 4)


VMEM_SPEC = pl.BlockSpec(memory_space=pltpu.VMEM)
SMEM_SPEC = pl.BlockSpec(memory_space=pltpu.SMEM)
MEGABYTE = 1 << 20


def on_chip(kernel, out_shape, scalars, *operands, scratch=(), megabytes=8, moved=1, place=VMEM_SPEC):
    return pl.pallas_call(
        kernel,
        out_shape=out_shape,
        in_specs=[SMEM_SPEC] * len(scalars) + [place] * len(operands),
        out_specs=jax.tree.map(lambda _: VMEM_SPEC, out_shape),
        scratch_shapes=scratch,
        compiler_params=pltpu.CompilerParams(vmem_limit_bytes=megabytes * MEGABYTE),
        cost_estimate=pl.CostEstimate(flops=0, bytes_accessed=moved * MEGABYTE, transcendentals=0),
    )(*scalars, *operands)


def norm_kernel(position_hbm, token_hbm, gain_hbm, out_ref, position_ref, token_ref, gain_ref, arrivals):
    pairs = ((token_hbm, token_ref), (gain_hbm, gain_ref), (position_hbm, position_ref))
    copies = [pltpu.make_async_copy(source, target, arrivals.at[n]) for n, (source, target) in enumerate(pairs)]
    for copy in copies:
        copy.start()
    core = lax.axis_index("inp")
    half = token_ref.shape[1] // 2
    rows = position_ref.shape[0]
    own = pl.ds(pl.multiple_of(core * half, 128), half)
    copies[0].wait()
    values = token_ref[...].astype(jnp.float32)
    factor = lax.rsqrt(jnp.mean(values * values, axis=-1, keepdims=True) + 1e-05)
    copies[1].wait()
    out_ref[:, :half] = (token_ref[:, own].astype(jnp.float32) * factor * gain_ref[:, own]).astype(jnp.bfloat16)
    shape = (token_ref.shape[0], 128)
    row = lax.broadcasted_iota(jnp.int32, shape, 0) % rows
    lane = lax.broadcasted_iota(jnp.int32, shape, 1)
    tag = jnp.zeros(shape, jnp.int32)
    copies[2].wait()
    for r in range(rows):
        place = position_ref[r]
        tag = jnp.where(row == r, jnp.where(lane == 0, place // 128, place % 128), tag)
    out_ref[:, half:] = tag.astype(jnp.float32).astype(jnp.bfloat16)


def fetch_kernel(starts, *refs):
    count = (len(refs) - 2) // 2
    mark_ref, arrivals = refs[-2:]
    copies = []
    for n in range(count):
        source, target = refs[n], refs[count + n]
        size = target.shape[0] // 4
        for part in range(4):
            there, here = pl.ds(starts[n] + part * size, size), pl.ds(part * size, size)
            copies.append(pltpu.make_async_copy(source.at[there], target.at[here], arrivals.at[n, part]))
    for copy in copies:
        copy.start()
    mark_ref[...] = jnp.zeros_like(mark_ref)
    for copy in copies:
        copy.wait()


def distant(array):
    return pltpu.with_memory_space_constraint(array, pltpu.HBM)


ANYWHERE = pl.BlockSpec(memory_space=pl.ANY)


def fetched(*parts):
    shapes = [(rows,) + array.shape[1:] for array, _, rows in parts]
    *near, mark = pl.pallas_call(
        functools.partial(fetch_kernel, [start for _, start, _ in parts]),
        out_shape=[pltpu.VMEM(shape, part[0].dtype) for shape, part in zip(shapes, parts)]
        + [jax.ShapeDtypeStruct((8, 128), jnp.float32)],
        in_specs=[ANYWHERE] * len(parts),
        out_specs=[VMEM_SPEC] * (len(parts) + 1),
        scratch_shapes=[pltpu.SemaphoreType.DMA((len(parts), 4))],
        compiler_params=pltpu.CompilerParams(vmem_limit_bytes=MEGABYTE),
        cost_estimate=pl.CostEstimate(
            flops=0, bytes_accessed=sum(2 * math.prod(shape) for shape in shapes), transcendentals=0
        ),
    )(*[distant(array) for array, _, _ in parts])
    return near, mark


def after_kernel(*refs):
    pass


def after(block, *others):
    return pl.pallas_call(
        after_kernel,
        out_shape=jax.ShapeDtypeStruct(block.shape, block.dtype),
        in_specs=[ANYWHERE] * (1 + len(others)),
        out_specs=ANYWHERE,
        input_output_aliases={0: 0},
        compiler_params=pltpu.CompilerParams(vmem_limit_bytes=MEGABYTE),
    )(block, *others)


def stack_rows(pieces, rows_ref):
    core = lax.axis_index("inp")
    rows = pieces[0].shape[0]
    for n, piece in enumerate(pieces):
        offset = jnp.where(core == 0, OFFSETS[0][n] ^ 4, OFFSETS[1][n])
        rows_ref[pl.ds(pl.multiple_of(offset * rows, rows), rows), :] = piece[...]


def multiply(rows_ref, weights, at, block):
    total, first = 0.0, 0
    for weight in weights:
        depth = weight.shape[0]
        total += jnp.dot(
            rows_ref[:, first : first + depth], weight[:, at : at + block], preferred_element_type=jnp.float32
        )
        first += depth
    return total


def project_kernel(*refs):
    pieces, key_ref, value_ref, queries = refs[:8], refs[8], refs[9], refs[10:-4]
    given_ref, kept_ref, tag_ref, rows_ref = refs[-4:]
    stack_rows(pieces, rows_ref)
    count, depth = given_ref.shape[0], key_ref.shape[0]
    tag_ref[...] = rows_ref[count:, depth:].astype(jnp.float32)
    first = 0
    for weights in (queries, (key_ref,), (value_ref,)):
        width = weights[0].shape[1]
        block = min(256, width)
        for at in range(0, width, block):
            sums = multiply(rows_ref, weights, at, block)
            given_ref[:, first + at : first + at + block] = sums[:count]
            kept_ref[:, first + at : first + at + block] = sums[count:]
        first += width


def mix_kernel(*refs):
    pieces, weights, (given_ref, kept_ref, rows_ref) = refs[:8], refs[8:-3], refs[-3:]
    stack_rows(pieces, rows_ref)
    count = given_ref.shape[0]
    for at in range(0, weights[0].shape[1], 256):
        sums = multiply(rows_ref, weights, at, 256)
        given_ref[:, at : at + 256] = sums[:count]
        kept_ref[:, at : at + 256] = sums[count:]


def turn_kernel(kept_ref, arrived_ref, cosine_ref, sine_ref, *out_refs):
    rows = out_refs[0].shape[0]
    heads = kept_ref.shape[1] // HEAD_SIZE
    for n, out_ref in enumerate(out_refs):
        here = pl.ds(n * rows, rows)
        cosine, sine = cosine_ref[here, :], sine_ref[here, :]
        for head in range(heads):
            columns = slice(head * HEAD_SIZE, (head + 1) * HEAD_SIZE)
            total = kept_ref[here, columns] + arrived_ref[here, columns]
            if head < heads - 1:
                total = total * cosine + pltpu.roll(total, HEAD_SIZE // 2, 1) * sine
            out_ref[:, columns] = total.astype(jnp.bfloat16)


def round_kernel(kept_ref, arrived_ref, *out_refs):
    rows = out_refs[0].shape[0]
    for n, out_ref in enumerate(out_refs):
        total = kept_ref[pl.ds(n * rows, rows), :] + arrived_ref[pl.ds(n * rows, rows), :]
        out_ref[...] = total.astype(jnp.bfloat16)


def place_kernel(*refs):
    pieces, out_ref = refs[:8], refs[8]
    core = lax.axis_index("inp")
    width = pieces[0].shape[1]
    for n, piece in enumerate(pieces):
        its_core = core if n < 4 else 1 - core
        start = pl.multiple_of((its_core * 4 + place_of(n % 4)) * width, width)
        out_ref[:, pl.ds(start, width)] = piece[...]


def attend_kernel(length_ref, *refs):
    received, refs = refs[:4], refs[4:]
    keys, values, out_ref, query_rows, fresh_keys, fresh_values, scores = refs
    rows, columns = keys.shape[0], keys.shape[1]
    group = query_rows.shape[2]
    steps = received[0].shape[0] // rows
    asking = steps * group
    for place in range(4):
        block = received[place][...].astype(jnp.float32)
        head = place_of(place)
        for g in range(group):
            query_rows[head, :, g, :] = block[:, g * HEAD_SIZE : (g + 1) * HEAD_SIZE]
        for step in range(steps):
            here = slice(step * rows, (step + 1) * rows)
            fresh_keys[:, step * 4 + head, :] = block[here, group * HEAD_SIZE : (group + 1) * HEAD_SIZE]
            fresh_values[:, step * 4 + head, :] = block[here, (group + 1) * HEAD_SIZE :]
    lane = lax.broadcasted_iota(jnp.int32, (asking, 128), 1)
    own_step = lax.broadcasted_iota(jnp.int32, (asking, 128), 0) // group
    own_lanes = [lane % 4 == head for head in range(4)]
    open_to = (lane < 4 * steps) & (lane // 4 <= own_step)
    across = (((1,), (1,)), ((), ()))
    padding = jnp.zeros((128 - 4 * steps, HEAD_SIZE), jnp.float32)

    def compact(product):
        parts = [product[head * asking : (head + 1) * asking] for head in range(4)]
        return jnp.where(own_lanes[0], parts[0], jnp.where(own_lanes[1], parts[1], jnp.where(own_lanes[2], parts[2], parts[3])))

    def by_head(values, combine):
        for shift in (4, 8, 16, 32, 64):
            values = combine(values, pltpu.roll(values, shift, 1))
        return values

    maxima = []
    for r in range(rows):
        queries = jnp.concatenate(
            [query_rows[head, step * rows + r] for head in range(4) for step in range(steps)]
        ).astype(jnp.bfloat16)
        fresh = jnp.concatenate([fresh_keys[r], padding]).astype(jnp.bfloat16)
        product = lax.dot_general(queries, fresh, across, preferred_element_type=jnp.float32)
        highest = jnp.where(open_to, compact(product), -jnp.inf)
        scores[r, :, columns:] = highest
        for at in range(0, columns, 256):
            product = lax.dot_general(
                queries, keys[r, at : at + 256, :], across, preferred_element_type=jnp.float32
            )
            for start in (at, at + 128):
                part = compact(product[:, start - at : start - at + 128])
                part = jnp.where(lane < 4 * length_ref[r] - start, part, -jnp.inf)
                scores[r, :, start : start + 128] = part
                highest = jnp.maximum(highest, part)
        maxima.append(highest)
    maxima = by_head(jnp.concatenate(maxima), jnp.maximum)
    factor = HEAD_SIZE ** (-0.5) * math.log2(math.e)
    totals = []
    for r in range(rows):
        highest = maxima[r * asking : (r + 1) * asking]
        total = jnp.zeros_like(highest)
        for start in range(0, columns + 128, 128):
            part = jnp.exp2((scores[r, :, start : start + 128] - highest) * factor)
            scores[r, :, start : start + 128] = part
            total += part
        totals.append(total)
    shares = 1.0 / by_head(jnp.concatenate(totals), jnp.add)
    for r in range(rows):
        share = shares[r * asking : (r + 1) * asking]
        spread = []
        for start in range(0, columns + 128, 128):
            part = scores[r, :, start : start + 128] * share
            spread.append(
                jnp.concatenate([jnp.where(own_lanes[head], part, 0.0) for head in range(4)]).astype(jnp.bfloat16)
            )
        fresh = jnp.concatenate([fresh_values[r], padding]).astype(jnp.bfloat16)
        result = jnp.dot(spread[-1], fresh, preferred_element_type=jnp.float32)
        result += jnp.dot(jnp.concatenate(spread[:-1], axis=1), values[r], preferred_element_type=jnp.float32)
        for n in range(4 * steps):
            query_rows[n // steps, n % steps * rows + r] = result[n * group : (n + 1) * group]
    for head in range(4):
        for g in range(group):
            start = (head * group + g) * HEAD_SIZE
            out_ref[:, start : start + HEAD_SIZE] = query_rows[head, :, g, :].astype(jnp.bfloat16)


def attend(received, cache_keys, cache_values, lengths):
    shape = jax.ShapeDtypeStruct
    rows, columns, _ = cache_keys.shape
    key_heads = 4
    count, width = received[0].shape
    group = width // HEAD_SIZE - 2
    fresh = count // rows * key_heads
    return pl.pallas_call(
        attend_kernel,
        out_shape=shape((count, key_heads * group * HEAD_SIZE), jnp.bfloat16),
        in_specs=[SMEM_SPEC] + [VMEM_SPEC] * 6,
        out_specs=VMEM_SPEC,
        scratch_shapes=[
            pltpu.VMEM((key_heads, count, group, HEAD_SIZE), jnp.float32),
            pltpu.VMEM((rows, fresh, HEAD_SIZE), jnp.float32),
            pltpu.VMEM((rows, fresh, HEAD_SIZE), jnp.float32),
            pltpu.VMEM((rows, count // rows * group, columns + 128), jnp.float32),
        ],
        compiler_params=pltpu.CompilerParams(vmem_limit_bytes=6 * MEGABYTE),
        cost_estimate=pl.CostEstimate(flops=0, bytes_accessed=12 * MEGABYTE, transcendentals=0),
    )(lengths, *received, resident(cache_keys), resident(cache_values))


def resident(array):
    return pltpu.with_memory_space_constraint(array, pltpu.VMEM)


def eight_chip_body(
    tokens, norm_gain, query_weight, key_matrix, value_matrix, output_weight, cache_keys, cache_values, lengths, positions
):
    steps, rows, width = tokens.shape
    count = steps * rows
    half = width // 2
    core = lax.axis_index("inp")
    query_cols = query_weight.shape[1]
    qkv_cols = query_cols + 2 * key_matrix.shape[1]
    shape = jax.ShapeDtypeStruct
    own = on_chip(
        norm_kernel,
        shape((count, half + 128), jnp.bfloat16),
        (),
        distant(positions),
        distant(tokens.reshape(count, width)),
        distant(norm_gain.reshape(1, width)),
        scratch=[
            pltpu.SMEM((rows,), jnp.int32),
            pltpu.VMEM((count, width), jnp.bfloat16),
            pltpu.VMEM((1, width), jnp.float32),
            pltpu.SemaphoreType.DMA((3,)),
        ],
        place=pl.BlockSpec(memory_space=pltpu.HBM),
    )
    depth = query_weight.shape[0]
    (query_first, near_key, near_value,), early = fetched((query_weight, 0, depth * 2048 // 4096), (key_matrix, 0, depth), (value_matrix, 0, depth))
    (query_second,), late = fetched((query_weight, depth * 2048 // 4096, depth - depth * 2048 // 4096))
    (near_keys, near_values), cache_mark = fetched(
        (cache_keys.reshape(rows, -1, HEAD_SIZE), 0, rows), (cache_values.reshape(rows, -1, HEAD_SIZE), 0, rows)
    )
    blocks = gather_blocks(own, early, late)
    given, kept, tags = on_chip(
        project_kernel,
        [shape((4 * count, qkv_cols), jnp.float32)] * 2 + [shape((4 * count, 128), jnp.float32)],
        (),
        *blocks,
        resident(near_key),
        resident(near_value),
        resident(query_first),
        resident(query_second),
        scratch=[pltpu.VMEM((8 * count, half + 128), jnp.bfloat16)],
    )
    arrived = swap_cores(given)
    frequency = jnp.exp(
        -math.log(500000.0) * 2.0 * jnp.arange(HEAD_SIZE // 2, dtype=jnp.float32) / HEAD_SIZE
    )
    step = (jnp.arange(4 * count) // rows % steps).astype(jnp.float32)
    angles = (tags[:, 0] * 128.0 + tags[:, 1] + step)[:, None] * frequency
    cosine, sine = jnp.cos(angles), jnp.sin(angles)
    outgoing = on_chip(
        turn_kernel,
        [shape((count, qkv_cols), jnp.bfloat16)] * 4,
        (),
        kept,
        arrived,
        jnp.concatenate([cosine, cosine], axis=-1),
        jnp.concatenate([-sine, sine], axis=-1),
    )
    attended = attend(hand_out(outgoing), near_keys, near_values, lengths)
    (output_first,), early = fetched((output_weight, 0, depth * 2048 // 4096))
    (output_second,), late = fetched((output_weight, depth * 2048 // 4096, depth - depth * 2048 // 4096))
    blocks = gather_blocks(attended, early, late)
    mix_cols = output_weight.shape[1]
    given, kept = on_chip(
        mix_kernel,
        [shape((4 * count, mix_cols), jnp.float32)] * 2,
        (),
        *blocks,
        resident(output_first),
        resident(output_second),
        scratch=[pltpu.VMEM((8 * count, half), jnp.bfloat16)],
    )
    outgoing = on_chip(
        round_kernel, [shape((count, mix_cols), jnp.bfloat16)] * 4, (), kept, swap_cores(given)
    )
    own_half = hand_out(outgoing)
    mixed = on_chip(
        place_kernel,
        shape((count, width), jnp.bfloat16),
        (),
        *own_half,
        *map(swap_cores, own_half),
    )
    return mixed.reshape(steps, rows, width)


def body(
    tokens,
    norm_gain,
    query_weight,
    key_matrix,
    value_matrix,
    output_weight,
    cache_keys,
    stored_cache_values,
    lengths,
    positions,
):
    normalized_input = rms_normed(tokens, norm_gain)
    key_list = []
    value_list = []
    results = []
    for token_step in range(2):
        queries, incoming_keys, incoming_values = project(
            normalized_input[token_step : token_step + 1],
            query_weight,
            key_matrix,
            value_matrix,
            positions,
            token_step,
        )
        key_list.append(incoming_keys[0])
        value_list.append(incoming_values[0])
        attended = attend_one(
            queries[0],
            jnp.stack(key_list),
            jnp.stack(value_list),
            cache_keys,
            stored_cache_values,
            lengths,
        )
        results.append(mix_out(attended[None], output_weight)[0])
    return jnp.stack(results)


def solution(mesh):
    placed = (
        P(None, ("group", "out"), None),
        P(),
        P("inp", "out"),
        P("inp", "out"),
        P("inp", "out"),
        P("inp", "out"),
        P(("group", "out"), None, "inp", None),
        P(("group", "out"), None, "inp", None),
        P(("group", "out")),
        P(("group", "out")),
    )
    chosen = eight_chip_body if (mesh.shape["out"], mesh.shape["inp"]) == (8, 2) else body
    return jax.shard_map(
        chosen, mesh=mesh, in_specs=placed, out_specs=P(None, ("group", "out"), None), check_vma=False
    )
```
